256 devices in a mesh: fsdp: 16 (over z, core), dp: 4 (over y), ctx: 4 (over x).
Axes of the slice: x: 4, y: 4, z: 8, core: 2. Of those that a mesh axis runs over, the one named last changes fastest.
Arguments:
- weights: bfloat16 [4, 512, 8192], P(None, None, 'fsdp'), may hold values from -0.119628906 to 0.119628906
- momentum: bfloat16 [4, 512, 8192], P(None, None, 'fsdp'), may hold values from -400 to 400, as said below
- gradient: bfloat16 [4, 512, 8192], P(None, None, 'fsdp'), may hold values from -400 to 400, as said below
- logit_max: float32 [4, 4, 61, 32], P('dp', 'ctx'), may hold values from 0.2 to 600, as said below
- layer_of: int32 [4], replicated, may hold values from 0 to 60
Outputs:
- new_weights: bfloat16 [4, 512, 8192], P(None, None, 'fsdp')
- new_momentum: bfloat16 [4, 512, 8192], P(None, None, 'fsdp')
The draws below stay inside these ranges and needn't reach their ends.
Inputs may be any that keep to these rules, and one draw needn't show every extreme that they name: `momentum`: entries of order one to some hundred, rows and columns of different scales. `gradient`: entries of order one to some hundred, rows and columns of different scales. `logit_max`: positive.
All inputs are finite; a program needn't handle non-finite values.
Results may differ from the reference program's by a relative error of at most 0.0062.
Values may be sent and summed in bfloat16 or wider, within the bound.
No kernel may reach another device: no remote copies, remote signals or barrier semaphores. Data moves between devices by JAX's collectives and lax.ppermute only.
A program may use at most 64 MiB of HBM per device.

```python
import math
import jax
import jax.numpy as jnp
from jax import lax

RANK = 512
HEADS = 32
KNOPE = 128
VDIM = 128
LAYERS = 61
ITERS = 5
DATA_REPS = 4
CTX_PARTS = 4
MATS = 4
COLS = 8192


def spread_values(key, low_scale, high_scale, base):
    row_key, column_key = jax.random.split(key, 2)
    row_scale = jnp.exp(jax.random.uniform(row_key, (MATS, RANK, 1), jnp.float32, math.log(low_scale), math.log(high_scale)))
    column_scale = jnp.exp(jax.random.uniform(column_key, (MATS, 1, COLS), jnp.float32, math.log(low_scale), math.log(high_scale)))
    ramp = jnp.exp(math.log(3.0) * jnp.arange(COLS, dtype=jnp.float32) / COLS)
    return base * row_scale * column_scale * ramp[None, None, :]


def draw_momentum(key, part):
    key = jax.random.fold_in(key, 11)
    base_key, rest_key = jax.random.split(key)
    base = jnp.clip(jax.random.normal(base_key, (MATS, RANK, COLS), jnp.float32), -5.0, 5.0)
    return spread_values(rest_key, 0.3, 3.0, base).astype(jnp.bfloat16)


def draw_gradient(key, part):
    key = jax.random.fold_in(key, 12)
    base_key, rest_key = jax.random.split(key)
    base = jnp.clip(jax.random.normal(base_key, (MATS, RANK, COLS), jnp.float32), -5.0, 5.0)
    return spread_values(rest_key, 0.3, 3.0, base).astype(jnp.bfloat16)


def draw_logit_max(key, part):
    key = jax.random.fold_in(key, 13)
    level_key, spread_key = jax.random.split(key)
    level = jnp.exp(jax.random.uniform(level_key, (1, 1, LAYERS, HEADS), jnp.float32, math.log(20.0), math.log(600.0)))
    spread = jnp.exp(jax.random.uniform(spread_key, (DATA_REPS, CTX_PARTS, LAYERS, HEADS), jnp.float32, math.log(0.01), 0.0))
    return jnp.clip(level * spread, 0.2, 600.0)


def place_ends(result, own_key, smallest, largest):
    index_at = [jax.random.randint(jax.random.fold_in(own_key, axis), (), 0, length) for axis, length in enumerate(result.shape)]
    widest = result.shape.index(max(result.shape))
    next_to = index_at[:widest] + [(index_at[widest] + 1) % result.shape[widest]] + index_at[widest + 1:]
    return result.at[tuple(index_at)].set(smallest).at[tuple(next_to)].set(largest)


def block_scale(own_key, extent, shards, low, largest):
    loudness = 1.0
    for axis_at, parts in shards:
        heights = jax.random.uniform(jax.random.fold_in(jax.random.fold_in(own_key, 6), axis_at), (parts,), jnp.float32, low / len(shards), largest / len(shards))
        loudness = loudness * jnp.repeat(jnp.exp(heights), extent[axis_at] // parts).reshape((-1,) + (1,) * (len(extent) - 1 - axis_at))
    return loudness


def gaussian(own_key, shape, scale, most, shards=(), kind=jnp.bfloat16):
    values = scale * jax.random.normal(own_key, shape, jnp.float32)
    if shards:
        values = values * block_scale(own_key, shape, shards, -0.22, 0.18)
    return jnp.clip(values, -most, most).astype(kind)


def setup_inputs(seed: int = 0) -> dict:
    key_of = jax.random.split(jax.random.key(seed), 6)
    weights = gaussian(key_of[0], (MATS, RANK, COLS), 0.02, 0.119628906, ((2, 16),))
    momentum = draw_momentum(jax.random.fold_in(key_of[5], 71), 0)
    gradient = draw_gradient(jax.random.fold_in(key_of[5], 71), 0)
    logit_max = draw_logit_max(jax.random.fold_in(key_of[5], 71), 0)
    layer_of = place_ends(jax.random.randint(key_of[4], (MATS,), 0, LAYERS), jax.random.fold_in(key_of[4], 1), 0, LAYERS - 1).astype(jnp.int32)
    return {"weights": weights, "momentum": momentum, "gradient": gradient, "logit_max": logit_max, "layer_of": layer_of}


quintic_a = 3.4445
quintic_b = -4.775
quintic_c = 2.0315
momentum_decay = 0.95
step_size = 0.1
clip_limit = 100.0
norm_eps = 1e-07
rms_factor = 0.2

def newton_gram(gram_now):
    highest = lax.Precision.HIGHEST
    identity = jnp.eye(gram_now.shape[0], dtype=jnp.float32)
    factors = identity
    for iteration in range(ITERS):
        square = jnp.dot(gram_now, gram_now, precision=highest)
        factor = quintic_a * identity + quintic_b * gram_now + quintic_c * square
        left_side = jnp.dot(factor, gram_now, precision=highest)
        gram_now = jnp.dot(left_side, factor, precision=highest)
        if iteration == 0:
            factors = factor
        else:
            factors = jnp.dot(factor, factors, precision=highest)
    return factors

def reference(weights, momentum, gradient, logit_max, layer_of):
    new_momentum = (momentum_decay * momentum.astype(jnp.float32) + gradient.astype(jnp.float32)).astype(jnp.bfloat16)
    peaks = lax.optimization_barrier(jnp.max(logit_max, axis=(0, 1)))
    chosen = peaks[layer_of.astype(jnp.int32)]
    scales = jnp.sqrt(jnp.minimum(1.0, clip_limit / chosen))
    columns = jnp.arange(COLS, dtype=jnp.int32)
    head_ids = columns // (KNOPE + VDIM)
    key_column = columns % (KNOPE + VDIM) < KNOPE
    column_scale = jnp.where(key_column[None, :], scales[:, head_ids], 1.0)
    results = []
    for index in range(MATS):
        matrix = new_momentum[index]
        gram_now = jnp.dot(matrix, matrix.T, preferred_element_type=jnp.float32)
        norm_value = jnp.sqrt(jnp.trace(gram_now)) + norm_eps
        scaled = (matrix.astype(jnp.float32) / norm_value).astype(jnp.bfloat16)
        factors = newton_gram(gram_now / (norm_value * norm_value))
        orthogonal = jnp.dot(factors.astype(jnp.bfloat16), scaled, preferred_element_type=jnp.float32)
        update = rms_factor * math.sqrt(max(RANK, COLS)) * orthogonal
        fresh_matrix = (weights[index].astype(jnp.float32) - step_size * update) * column_scale[index][None, :]
        results.append(fresh_matrix.astype(jnp.bfloat16))
    return (jnp.stack(results, axis=0), new_momentum)
```

```python
import functools
import math

import jax
import jax.numpy as jnp
from jax import lax
from jax.experimental import pallas as pl
from jax.experimental.pallas import tpu as pltpu
from jax.sharding import PartitionSpec as P

KNOPE = 128
VDIM = 128
ITERS = 5

quintic_a = 3.4445
quintic_b = -4.775
quintic_c = 2.0315
momentum_decay = 0.95
step_size = 0.1
clip_limit = 100.0
norm_eps = 1e-07
rms_factor = 0.2

BLOCK = 128
BLOCKS = 4
PART = 160
TAIL = 8
HALF = 640
END = 16
UPPER = [(row, column) for row in range(BLOCKS) for column in range(row, BLOCKS)]


def decayed(momentum, gradient):
    return (momentum_decay * momentum.astype(jnp.float32) + gradient.astype(jnp.float32)).astype(jnp.bfloat16)


def aligned(index, to):
    return pl.multiple_of(index * to, to)


def partial_gram_kernel(momentum_ref, gradient_ref, keep_ref, send_ref, momentum, gradient, fresh, packed, arrived):
    matrix, dp_at, core = lax.axis_index("ctx"), lax.axis_index("dp"), lax.rem(lax.axis_index("fsdp"), 2)
    copies = []
    for at in (0, 2, 1):
        rows = pl.ds(aligned(lax.rem(dp_at + at, BLOCKS), BLOCK), BLOCK)
        pair = [
            pltpu.make_async_copy(source.at[matrix, rows], target.at[at], arrived.at[side, at])
            for side, (source, target) in enumerate(((momentum_ref, momentum), (gradient_ref, gradient)))
        ]
        for copy in pair:
            copy.start()
        copies.append((at, pair))
    for at, pair in copies:
        for copy in pair:
            copy.wait()
        fresh[at * BLOCK : (at + 1) * BLOCK, :] = decayed(momentum[at], gradient[at])

    def gram(left, right):
        return lax.dot_general(left, right, (((1,), (1,)), ((), ())), preferred_element_type=jnp.float32)

    early = dp_at < BLOCKS // 2
    far_rows = jnp.where(early, 0, 5)
    far_columns = jnp.where(early, 2, 0)
    packed[2 * BLOCK :, :] = gram(
        fresh[pl.ds(aligned(far_rows, BLOCK // 2), BLOCK // 2), :], fresh[pl.ds(aligned(far_columns, BLOCK), BLOCK), :]
    )
    packed[0:BLOCK, :] = gram(fresh[0:BLOCK, :], fresh[0:BLOCK, :])
    packed[BLOCK : 2 * BLOCK, :] = gram(fresh[0:BLOCK, :], fresh[BLOCK : 2 * BLOCK, :])
    keep_ref[...] = packed[pl.ds(aligned(core, PART), PART), :]
    send_ref[...] = packed[pl.ds(aligned(1 - core, PART), PART), :]


def partial_gram(momentum, gradient):
    rank, cols = momentum.shape[1:]
    shape = jax.ShapeDtypeStruct((PART, BLOCK), jnp.float32)
    blocks = pltpu.VMEM((3, BLOCK, cols), jnp.bfloat16)
    return pl.pallas_call(
        partial_gram_kernel,
        out_shape=(shape, shape),
        in_specs=[pl.BlockSpec(memory_space=pl.ANY)] * 2,
        out_specs=(pl.BlockSpec(memory_space=pltpu.VMEM),) * 2,
        scratch_shapes=[
            blocks,
            blocks,
            pltpu.VMEM((3 * BLOCK, cols), jnp.bfloat16),
            pltpu.VMEM((2 * PART, BLOCK), jnp.float32),
            pltpu.SemaphoreType.DMA((2, 3)),
        ],
        compiler_params=pltpu.CompilerParams(vmem_limit_bytes=62 * 2**20),
        cost_estimate=pl.CostEstimate(flops=4 * PART * BLOCK * cols, bytes_accessed=3 * rank * cols, transcendentals=0),
    )(momentum, gradient)


def split_in_two(value):
    high = value.astype(jnp.bfloat16)
    return high, (value - high.astype(jnp.float32)).astype(jnp.bfloat16)


def split_in_three(value):
    high = value.astype(jnp.bfloat16)
    rest = value - high.astype(jnp.float32)
    middle = rest.astype(jnp.bfloat16)
    return high, middle, (rest - middle.astype(jnp.float32)).astype(jnp.bfloat16)


def newton_kernel(*refs):
    (own, near, cross, far), rest = [refs[2 * at : 2 * at + 2] for at in range(BLOCKS)], refs[2 * BLOCKS :]
    first_ref, second_ref, peaks_ref, packed, stacks, a_now, pairs_q, pair_a, pair_b, pair_p = rest
    rank = pair_a.shape[1]
    mid = rank // 2
    dp_at, core = lax.axis_index("dp"), lax.rem(lax.axis_index("fsdp"), 2)
    for turn, pair in ((0, own), (1 + 2 * core, near), (3 - 2 * core, cross), (2, far)):
        for side, piece in enumerate(pair):
            half = core + side - 2 * core * side
            stacks[dp_at ^ turn, pl.ds(aligned(half, PART), PART), :] = piece[0:PART, :]
    peaks = jnp.maximum(jnp.maximum(own[0][PART:, :], near[0][PART:, :]), jnp.maximum(cross[0][PART:, :], far[0][PART:, :]))
    peaks_ref[...] = peaks

    def own_block(block):
        return stacks[block, 0:BLOCK, :]

    def beside(block):
        return stacks[block, BLOCK : 2 * BLOCK, :]

    eye = lax.broadcasted_iota(jnp.int32, (BLOCK, BLOCK), 0) == lax.broadcasted_iota(jnp.int32, (BLOCK, BLOCK), 1)
    diagonal = (own_block(0) + own_block(1)) + (own_block(2) + own_block(3))
    norm = jnp.sqrt(jnp.full((1, 1), jnp.sum(jnp.where(eye, diagonal, 0.0)), jnp.float32)) + norm_eps
    inverse = 1.0 / (norm * norm)

    def place(row, column, value):
        a_now[row * BLOCK : (row + 1) * BLOCK, column * BLOCK : (column + 1) * BLOCK] = value

    for block in range(BLOCKS):
        place(block, block, own_block(block) * inverse)
        after = (block + 1) % BLOCKS
        place(block, after, beside(block) * inverse)
        place(after, block, beside(block).T * inverse)
    for block in range(2):
        far_block = jnp.concatenate([stacks[block, 2 * BLOCK :, :], stacks[block + 2, 2 * BLOCK :, :]], axis=0) * inverse
        place(block, block + 2, far_block)
        place(block + 2, block, far_block.T)

    strips = [slice(0, mid), slice(mid, rank)]
    rows_at = lax.broadcasted_iota(jnp.int32, (rank, mid), 0)
    columns_at = lax.broadcasted_iota(jnp.int32, (rank, mid), 1)
    shifts = [jnp.where(rows_at == columns_at + strip.start, quintic_a, 0.0) for strip in strips]
    dot = functools.partial(jnp.dot, preferred_element_type=jnp.float32)

    def keep(pair, strip, value):
        pair[0, :, strip], pair[1, :, strip] = split_in_two(value)

    def product(left, right, strip):
        return dot(left[0], right[0, :, strip]) + (dot(left[0], right[1, :, strip]) + dot(left[1], right[0, :, strip]))

    for strip in strips:
        keep(pair_a, strip, a_now[:, strip])
    for iteration in range(ITERS):
        pair_q = pairs_q.at[iteration % 2]
        for strip, shift in zip(strips, shifts):
            square = product(pair_a, pair_a, strip)
            keep(pair_q, strip, shift + quintic_b * a_now[:, strip] + quintic_c * square)
        if iteration == ITERS - 1:
            break
        for strip in strips:
            keep(pair_b, strip, product(pair_q, pair_a, strip))
        if iteration == 0:
            pair_p[...] = pair_q[...]
        else:
            keep(pair_p, strips[0], product(pair_q, pair_p, strips[0]))
        for strip in strips:
            a_now[:, strip] = product(pair_q, pair_b, strip)
            keep(pair_a, strip, a_now[:, strip])
        if iteration > 0:
            keep(pair_p, strips[1], product(pair_q, pair_p, strips[1]))
    for strip in strips:
        a_now[:, strip] = product(pair_q, pair_p, strip)
    for at, (row, column) in enumerate(UPPER):
        block = a_now[row * BLOCK : (row + 1) * BLOCK, column * BLOCK : (column + 1) * BLOCK]
        at_row = at % (HALF // BLOCK) * BLOCK
        packed[at // (HALF // BLOCK), at_row : at_row + BLOCK, :] = block.astype(jnp.bfloat16)
    line = lax.broadcasted_iota(jnp.int32, (END, BLOCK), 0)
    spread = jnp.zeros((END, BLOCK), jnp.float32)
    for at, term in enumerate(split_in_three(norm)):
        spread = jnp.where(line == at, term.astype(jnp.float32), spread)
    for half in range(2):
        packed[half, HALF:, :] = spread.astype(jnp.bfloat16)
    first_ref[...] = packed[core]
    second_ref[...] = packed[1 - core]


def newton(parts, rank):
    whole = pl.BlockSpec(memory_space=pltpu.VMEM)
    pair = pltpu.VMEM((2, rank, rank), jnp.bfloat16)
    piece = jax.ShapeDtypeStruct((HALF + END, BLOCK), jnp.bfloat16)
    return pl.pallas_call(
        newton_kernel,
        out_shape=(piece, piece, jax.ShapeDtypeStruct((TAIL, BLOCK), jnp.float32)),
        in_specs=[whole] * len(parts),
        out_specs=(whole,) * 3,
        scratch_shapes=[
            pltpu.VMEM((2, HALF + END, BLOCK), jnp.bfloat16),
            pltpu.VMEM((BLOCKS, 2 * PART, BLOCK), jnp.float32),
            pltpu.VMEM((rank, rank), jnp.float32),
            pltpu.VMEM((2, 2, rank, rank), jnp.bfloat16),
            pair,
            pair,
            pair,
        ],
        compiler_params=pltpu.CompilerParams(vmem_limit_bytes=40 * 2**20),
        cost_estimate=pl.CostEstimate(flops=17 * 6 * rank**3, bytes_accessed=6 * rank * rank, transcendentals=0),
    )(*parts)


def last_kernel(update_scale, masks, weights_ref, momentum_ref, peaks_ref, first_ref, second_ref, *refs):
    out_ref, packed, factors, weights, momentum, fresh, arrived, left = refs[-8:]
    rank, cols = fresh.shape
    shard = lax.axis_index("fsdp")
    core = lax.rem(shard, 2)
    matrix = lax.axis_index("ctx") ^ (masks[0] + (masks[1] - masks[0]) * core)
    loads = [
        pltpu.make_async_copy(source.at[matrix], target, arrived.at[at])
        for at, (source, target) in enumerate(((momentum_ref, momentum), (weights_ref, weights)))
    ]
    for load in loads:
        load.start()
    packed[core] = first_ref[...]
    packed[1 - core] = second_ref[...]
    for at, (row, column) in enumerate(UPPER):
        at_row = at % (HALF // BLOCK) * BLOCK
        block = packed[at // (HALF // BLOCK), at_row : at_row + BLOCK, :]
        factors[row * BLOCK : (row + 1) * BLOCK, column * BLOCK : (column + 1) * BLOCK] = block
        if row != column:
            factors[column * BLOCK : (column + 1) * BLOCK, row * BLOCK : (row + 1) * BLOCK] = block.T
    end = first_ref[HALF:, :].astype(jnp.float32)
    norm = (end[0:1, 0:1] + end[1:2, 0:1]) + end[2:3, 0:1]
    heads = cols // (KNOPE + VDIM)
    column = lax.broadcasted_iota(jnp.int32, (1, cols), 1)
    lane = lax.broadcasted_iota(jnp.int32, (1, BLOCK), 1)
    column_peaks = jnp.full((1, cols), clip_limit, jnp.float32)
    for head in range(heads):
        place = matrix * (BLOCK // BLOCKS) + shard * heads + head
        peak = jnp.max(jnp.where(lane == place, peaks_ref[0:1, :], 0.0), axis=1, keepdims=True)
        first = head * (KNOPE + VDIM)
        column_peaks = jnp.where((column >= first) & (column < first + KNOPE), peak, column_peaks)
    scale = jnp.sqrt(jnp.minimum(1.0, clip_limit / column_peaks))
    loads[0].wait()
    momentum[...] = (momentum[...].astype(jnp.float32) / norm).astype(jnp.bfloat16)
    loads[1].wait()
    stores = []
    for at in range(BLOCKS):
        rows = slice(at * BLOCK, (at + 1) * BLOCK)
        orthogonal = jnp.dot(factors[rows, :], momentum[...], preferred_element_type=jnp.float32)
        value = (weights[rows, :].astype(jnp.float32) - step_size * (update_scale * orthogonal)) * scale
        fresh[rows, :] = value.astype(jnp.bfloat16)
        stores.append(pltpu.make_async_copy(fresh.at[rows], out_ref.at[matrix, rows], left.at[at]))
        stores[-1].start()
    for store in stores:
        store.wait()


def last_product(update_scale, masks, weights, momentum, peaks, pair, before):
    rank, cols = weights.shape[1:]
    whole, outside = pl.BlockSpec(memory_space=pltpu.VMEM), pl.BlockSpec(memory_space=pl.ANY)
    earlier = [] if before is None else [before]
    square, block = pltpu.VMEM((rank, rank), jnp.bfloat16), pltpu.VMEM((rank, cols), jnp.bfloat16)
    return pl.pallas_call(
        functools.partial(last_kernel, update_scale, masks),
        out_shape=jax.ShapeDtypeStruct(weights.shape, jnp.bfloat16),
        in_specs=[outside] * 2 + [whole] * 3 + [outside] * len(earlier),
        out_specs=outside,
        scratch_shapes=[
            pltpu.VMEM((2, HALF + END, BLOCK), jnp.bfloat16),
            square,
            block,
            block,
            block,
            pltpu.SemaphoreType.DMA((2,)),
            pltpu.SemaphoreType.DMA((BLOCKS,)),
        ],
        input_output_aliases={5: 0} if earlier else {},
        compiler_params=pltpu.CompilerParams(vmem_limit_bytes=24 * 2**20),
        cost_estimate=pl.CostEstimate(flops=2 * rank * rank * cols, bytes_accessed=6 * rank * cols, transcendentals=0),
    )(weights, momentum, peaks, *pair, *earlier)


def crossed(value, axis, mask):
    return lax.ppermute(value, axis, [(at, at ^ mask) for at in range(lax.axis_size(axis))])


def along_z(value, masks):
    pairs = [(at, (at // 2 ^ masks[at % 2]) * 2 + at % 2) for at in range(lax.axis_size("fsdp"))]
    return lax.ppermute(value, "fsdp", pairs)


def by_core(value, axis, masks):
    count = lax.axis_size(axis)
    pairs = [
        (shard * count + at, shard * count + (at ^ masks[shard % 2]))
        for shard in range(lax.axis_size("fsdp"))
        for at in range(count)
    ]
    return lax.ppermute(value, ("fsdp", axis), pairs)


def swapped(value):
    return crossed(value, "fsdp", 1)


def gather_halves(axis, half):
    near, cross = by_core(half, axis, (1, 3)), by_core(half, axis, (3, 1))
    far = by_core(near, axis, (3, 1))
    return (half, swapped(half)), (near, swapped(cross)), (cross, swapped(near)), (far, swapped(far))


def on_device(weights, momentum, gradient, logit_max, layer_of):
    rank, cols = weights.shape[1:]
    fsdp = lax.axis_size("fsdp")
    layers = logit_max.shape[2]

    keep, send = partial_gram(momentum, gradient)
    total = keep + swapped(send)

    layer_match = jnp.arange(layers, dtype=jnp.int32)[None, :] == layer_of[:, None]
    peaks = jnp.max(jnp.where(layer_match[:, :, None], logit_max[0, 0][None], 0.0), axis=1)
    peaks = jnp.broadcast_to(peaks.reshape(1, BLOCK), (TAIL, BLOCK))
    total = total + along_z(total, (1, 7))
    total = total + along_z(total, (3, 1))
    peaks = jnp.maximum(peaks, crossed(peaks, "ctx", 1))
    total, peaks = lax.optimization_barrier((total, peaks))
    total = total + along_z(total, (7, 3))
    peaks = jnp.maximum(peaks, crossed(peaks, "ctx", 3))
    new_momentum = decayed(momentum, gradient)
    total, new_momentum = lax.optimization_barrier((total, new_momentum))

    parts = gather_halves("dp", jnp.concatenate([total, peaks], axis=0))

    first, second, peaks = newton([piece for pair in parts for piece in pair], rank)
    update_scale = rms_factor * math.sqrt(max(rank, cols * fsdp))
    last = functools.partial(last_product, update_scale)
    near = tuple(by_core(piece, "ctx", (1, 3)) for piece in (first, second))
    new_weights = last((0, 0), weights, new_momentum, peaks, (first, second), None)
    near_first, new_weights = lax.optimization_barrier((near[0], new_weights))
    far = by_core(near_first, "ctx", (3, 1))
    cross = swapped(near[1]), swapped(near_first)
    new_weights = last((1, 3), weights, new_momentum, peaks, (near_first, near[1]), new_weights)
    far, new_weights = lax.optimization_barrier((far, new_weights))
    far = far, swapped(far)
    new_weights = last((3, 1), weights, new_momentum, peaks, cross, new_weights)
    new_weights = last((2, 2), weights, new_momentum, peaks, far, new_weights)
    return (new_weights, new_momentum)


def solution(mesh):
    in_specs = (
        P(None, None, "fsdp"),
        P(None, None, "fsdp"),
        P(None, None, "fsdp"),
        P("dp", "ctx", None, None),
        P(),
    )
    out_specs = (P(None, None, "fsdp"), P(None, None, "fsdp"))
    return jax.shard_map(
        on_device, mesh=mesh, in_specs=in_specs, out_specs=out_specs, check_vma=False
    )
```

```python
import functools
import math

import jax
import jax.numpy as jnp
from jax import lax
from jax.experimental import pallas as pl
from jax.experimental.pallas import tpu as pltpu
from jax.sharding import PartitionSpec as P

KNOPE = 128
VDIM = 128
ITERS = 5

quintic_a = 3.4445
quintic_b = -4.775
quintic_c = 2.0315
momentum_decay = 0.95
step_size = 0.1
clip_limit = 100.0
norm_eps = 1e-07
rms_factor = 0.2

BLOCK = 128
BLOCKS = 4
PART = 160
TAIL = 8
HALF = 640
END = 16
STRIP = 256
KEPT = [[(0, 0), (0, 1), (1, 1), (2, 0), (3, 0)], [(1, 2), (1, 3), (2, 2), (2, 3), (3, 3)]]


def decayed(momentum, gradient):
    return (momentum_decay * momentum.astype(jnp.float32) + gradient.astype(jnp.float32)).astype(jnp.bfloat16)


def aligned(index, to):
    return pl.multiple_of(index * to, to)


def partial_gram_kernel(momentum_ref, gradient_ref, keep_ref, send_ref, momentum, gradient, fresh, packed, arrived):
    matrix, dp_at, core = lax.axis_index("ctx"), lax.axis_index("dp"), lax.rem(lax.axis_index("fsdp"), 2)
    copies = []
    for at in (0, 2, 1):
        rows = pl.ds(aligned(lax.rem(dp_at + at, BLOCKS), BLOCK), BLOCK)
        pair = [
            pltpu.make_async_copy(source.at[matrix, rows], target.at[at], arrived.at[side, at])
            for side, (source, target) in enumerate(((momentum_ref, momentum), (gradient_ref, gradient)))
        ]
        for copy in pair:
            copy.start()
        copies.append((at, pair))
    for at, pair in copies:
        for copy in pair:
            copy.wait()
        fresh[at * BLOCK : (at + 1) * BLOCK, :] = decayed(momentum[at], gradient[at])

    def gram(left, right):
        return lax.dot_general(left, right, (((1,), (1,)), ((), ())), preferred_element_type=jnp.float32)

    early = dp_at < BLOCKS // 2
    far_rows = jnp.where(early, 0, 5)
    far_columns = jnp.where(early, 2, 0)
    packed[2 * BLOCK :, :] = gram(
        fresh[pl.ds(aligned(far_rows, BLOCK // 2), BLOCK // 2), :], fresh[pl.ds(aligned(far_columns, BLOCK), BLOCK), :]
    )
    packed[0:BLOCK, :] = gram(fresh[0:BLOCK, :], fresh[0:BLOCK, :])
    packed[BLOCK : 2 * BLOCK, :] = gram(fresh[0:BLOCK, :], fresh[BLOCK : 2 * BLOCK, :])
    keep_ref[...] = packed[pl.ds(aligned(core, PART), PART), :]
    send_ref[...] = packed[pl.ds(aligned(1 - core, PART), PART), :]


def partial_gram(momentum, gradient):
    rank, cols = momentum.shape[1:]
    shape = jax.ShapeDtypeStruct((PART, BLOCK), jnp.float32)
    blocks = pltpu.VMEM((3, BLOCK, cols), jnp.bfloat16)
    return pl.pallas_call(
        partial_gram_kernel,
        out_shape=(shape, shape),
        in_specs=[pl.BlockSpec(memory_space=pl.ANY)] * 2,
        out_specs=(pl.BlockSpec(memory_space=pltpu.VMEM),) * 2,
        scratch_shapes=[
            blocks,
            blocks,
            pltpu.VMEM((3 * BLOCK, cols), jnp.bfloat16),
            pltpu.VMEM((2 * PART, BLOCK), jnp.float32),
            pltpu.SemaphoreType.DMA((2, 3)),
        ],
        compiler_params=pltpu.CompilerParams(vmem_limit_bytes=62 * 2**20),
        cost_estimate=pl.CostEstimate(flops=4 * PART * BLOCK * cols, bytes_accessed=3 * rank * cols, transcendentals=0),
    )(momentum, gradient)


def split_in_two(value):
    high = value.astype(jnp.bfloat16)
    return high, (value - high.astype(jnp.float32)).astype(jnp.bfloat16)


def split_in_three(value):
    high = value.astype(jnp.bfloat16)
    rest = value - high.astype(jnp.float32)
    middle = rest.astype(jnp.bfloat16)
    return high, middle, (rest - middle.astype(jnp.float32)).astype(jnp.bfloat16)


def newton_kernel(*refs):
    parts, rest = [refs[2 * at : 2 * at + 2] for at in range(BLOCKS)], refs[2 * BLOCKS :]
    first_ref, second_ref, peaks_ref, packed, stacks, a_now, left_a, left_q, right_a, right_b, right_p = rest
    rank = a_now.shape[0]
    mid = rank // 2
    dp_at, core = lax.axis_index("dp"), lax.rem(lax.axis_index("fsdp"), 2)
    for turn, pair in enumerate(parts):
        for side, piece in enumerate(pair):
            half = core + side - 2 * core * side
            stacks[dp_at ^ turn, pl.ds(aligned(half, PART), PART), :] = piece[0:PART, :]
    peaks_ref[...] = functools.reduce(jnp.maximum, [pair[0][PART:, :] for pair in parts])

    def own_block(block):
        return stacks[block, 0:BLOCK, :]

    def beside(block):
        return stacks[block, BLOCK : 2 * BLOCK, :]

    eye = lax.broadcasted_iota(jnp.int32, (BLOCK, BLOCK), 0) == lax.broadcasted_iota(jnp.int32, (BLOCK, BLOCK), 1)
    diagonal = (own_block(0) + own_block(1)) + (own_block(2) + own_block(3))
    norm = jnp.sqrt(jnp.full((1, 1), jnp.sum(jnp.where(eye, diagonal, 0.0)), jnp.float32)) + norm_eps
    inverse = 1.0 / (norm * norm)

    def place(row, column, value):
        a_now[row * BLOCK : (row + 1) * BLOCK, column * BLOCK : (column + 1) * BLOCK] = value

    for block in range(BLOCKS):
        place(block, block, own_block(block) * inverse)
        after = (block + 1) % BLOCKS
        place(block, after, beside(block) * inverse)
        place(after, block, beside(block).T * inverse)
    for block in range(2):
        far_block = jnp.concatenate([stacks[block, 2 * BLOCK :, :], stacks[block + 2, 2 * BLOCK :, :]], axis=0) * inverse
        place(block, block + 2, far_block)
        place(block + 2, block, far_block.T)

    strips = [slice(0, mid), slice(mid, rank)]
    rows_at = lax.broadcasted_iota(jnp.int32, (rank, mid), 0)
    columns_at = lax.broadcasted_iota(jnp.int32, (rank, mid), 1)
    shifts = [jnp.where(rows_at == columns_at + strip.start, quintic_a, 0.0) for strip in strips]

    def keep(value, at, left=None, right=None):
        high, low = split_in_two(value)
        for turn, term in enumerate((high, low, high)):
            if left is not None:
                left[:, (3 * at + turn) * mid : (3 * at + turn + 1) * mid] = term
        for turn, term in enumerate((high, high, low)):
            if right is not None:
                for block, rows in enumerate(strips):
                    right[(3 * block + turn) * mid : (3 * block + turn + 1) * mid, strips[at]] = term[rows, :]

    def product(left, right, at):
        return jnp.dot(left[...], right[:, strips[at]], preferred_element_type=jnp.float32)

    for at, strip in enumerate(strips):
        keep(a_now[:, strip], at, left_a, right_a)
    for iteration in range(ITERS):
        for at, strip in enumerate(strips):
            factor = shifts[at] + quintic_b * a_now[:, strip] + quintic_c * product(left_a, right_a, at)
            keep(factor, at, left_q, right_p if iteration == 0 else None)
        if iteration == ITERS - 1:
            break
        for at in range(2):
            keep(product(left_q, right_a, at), at, None, right_b)
        if iteration > 0:
            keep(product(left_q, right_p, 0), 0, None, right_p)
        for at, strip in enumerate(strips):
            value = product(left_q, right_b, at)
            a_now[:, strip] = value
            keep(value, at, left_a, right_a)
        if iteration > 0:
            keep(product(left_q, right_p, 1), 1, None, right_p)
    for at, strip in enumerate(strips):
        a_now[:, strip] = product(left_q, right_p, at)
    for side, kept in enumerate(KEPT):
        for at, (row, column) in enumerate(kept):
            block = a_now[row * BLOCK : (row + 1) * BLOCK, column * BLOCK : (column + 1) * BLOCK]
            packed[side, at * BLOCK : (at + 1) * BLOCK, :] = block.astype(jnp.bfloat16)
    line = lax.broadcasted_iota(jnp.int32, (END, BLOCK), 0)
    spread = jnp.zeros((END, BLOCK), jnp.float32)
    for at, term in enumerate(split_in_three(norm)):
        spread = jnp.where(line == at, term.astype(jnp.float32), spread)
    for side in range(2):
        packed[side, HALF:, :] = spread.astype(jnp.bfloat16)
    first_ref[...] = packed[core]
    second_ref[...] = packed[1 - core]


def newton(parts, rank):
    whole = pl.BlockSpec(memory_space=pltpu.VMEM)
    left, right = pltpu.VMEM((rank, 3 * rank), jnp.bfloat16), pltpu.VMEM((3 * rank, rank), jnp.bfloat16)
    piece = jax.ShapeDtypeStruct((HALF + END, BLOCK), jnp.bfloat16)
    return pl.pallas_call(
        newton_kernel,
        out_shape=(piece, piece, jax.ShapeDtypeStruct((TAIL, BLOCK), jnp.float32)),
        in_specs=[whole] * len(parts),
        out_specs=(whole,) * 3,
        scratch_shapes=[
            pltpu.VMEM((2, HALF + END, BLOCK), jnp.bfloat16),
            pltpu.VMEM((BLOCKS, 2 * PART, BLOCK), jnp.float32),
            pltpu.VMEM((rank, rank), jnp.float32),
            left,
            left,
            right,
            right,
            right,
        ],
        compiler_params=pltpu.CompilerParams(vmem_limit_bytes=40 * 2**20),
        cost_estimate=pl.CostEstimate(flops=17 * 6 * rank**3, bytes_accessed=6 * rank * rank, transcendentals=0),
    )(*parts)


def last_kernel(update_scale, masks, weights_ref, momentum_ref, peaks_ref, first_ref, second_ref, *refs):
    out_ref, packed, factors, weights, momentum, fresh, arrived, left = refs[-8:]
    rank, cols = factors.shape[0], out_ref.shape[2]
    shard = lax.axis_index("fsdp")
    core = lax.rem(shard, 2)
    matrix = lax.axis_index("ctx") ^ (masks[0] + (masks[1] - masks[0]) * core)
    strips = [pl.ds(at * STRIP, STRIP) for at in range(cols // STRIP)]
    loads = [
        [
            pltpu.make_async_copy(source.at[matrix, :, strip], target.at[at], arrived.at[side, at])
            for side, (source, target) in enumerate(((momentum_ref, momentum), (weights_ref, weights)))
        ]
        for at, strip in enumerate(strips)
    ]
    for pair in loads:
        for load in pair:
            load.start()
    packed[core] = first_ref[...]
    packed[1 - core] = second_ref[...]
    for side, kept in enumerate(KEPT):
        for at, (row, column) in enumerate(kept):
            block = packed[side, at * BLOCK : (at + 1) * BLOCK, :]
            factors[row * BLOCK : (row + 1) * BLOCK, column * BLOCK : (column + 1) * BLOCK] = block
            if row != column:
                factors[column * BLOCK : (column + 1) * BLOCK, row * BLOCK : (row + 1) * BLOCK] = block.T
    end = first_ref[HALF:, :].astype(jnp.float32)
    inverse = 1.0 / ((end[0:1, 0:1] + end[1:2, 0:1]) + end[2:3, 0:1])
    heads = cols // (KNOPE + VDIM)
    column = lax.broadcasted_iota(jnp.int32, (1, cols), 1)
    lane = lax.broadcasted_iota(jnp.int32, (1, BLOCK), 1)
    column_peaks = jnp.full((1, cols), clip_limit, jnp.float32)
    for head in range(heads):
        place = matrix * (BLOCK // BLOCKS) + shard * heads + head
        peak = jnp.max(jnp.where(lane == place, peaks_ref[0:1, :], 0.0), axis=1, keepdims=True)
        first = head * (KNOPE + VDIM)
        column_peaks = jnp.where((column >= first) & (column < first + KNOPE), peak, column_peaks)
    scale = jnp.sqrt(jnp.minimum(1.0, clip_limit / column_peaks))
    stores = []
    for at, strip in enumerate(strips):
        loads[at][0].wait()
        start = (momentum[at].astype(jnp.float32) * inverse).astype(jnp.bfloat16)
        orthogonal = jnp.dot(factors[...], start, preferred_element_type=jnp.float32)
        loads[at][1].wait()
        value = weights[at].astype(jnp.float32) - step_size * (update_scale * orthogonal)
        fresh[at] = (value * scale[:, at * STRIP : (at + 1) * STRIP]).astype(jnp.bfloat16)
        stores.append(pltpu.make_async_copy(fresh.at[at], out_ref.at[matrix, :, strip], left.at[at]))
        stores[-1].start()
    for store in stores:
        store.wait()


def last_product(update_scale, masks, weights, momentum, peaks, pair, before):
    rank, cols = weights.shape[1:]
    whole, outside = pl.BlockSpec(memory_space=pltpu.VMEM), pl.BlockSpec(memory_space=pl.ANY)
    earlier = [] if before is None else [before]
    count = cols // STRIP
    square, block = pltpu.VMEM((rank, rank), jnp.bfloat16), pltpu.VMEM((count, rank, STRIP), jnp.bfloat16)
    return pl.pallas_call(
        functools.partial(last_kernel, update_scale, masks),
        out_shape=jax.ShapeDtypeStruct(weights.shape, jnp.bfloat16),
        in_specs=[outside] * 2 + [whole] * 3 + [outside] * len(earlier),
        out_specs=outside,
        scratch_shapes=[
            pltpu.VMEM((2, HALF + END, BLOCK), jnp.bfloat16),
            square,
            block,
            block,
            block,
            pltpu.SemaphoreType.DMA((2, count)),
            pltpu.SemaphoreType.DMA((count,)),
        ],
        input_output_aliases={5: 0} if earlier else {},
        compiler_params=pltpu.CompilerParams(vmem_limit_bytes=24 * 2**20),
        cost_estimate=pl.CostEstimate(flops=2 * rank * rank * cols, bytes_accessed=6 * rank * cols, transcendentals=0),
    )(weights, momentum, peaks, *pair, *earlier)


def crossed(value, axis, mask):
    return lax.ppermute(value, axis, [(at, at ^ mask) for at in range(lax.axis_size(axis))])


def along_z(value, mask):
    count = lax.axis_size("fsdp")
    zs = count // 2
    pairs = []
    for at in range(count):
        z_at, core = at // 2, at % 2
        partner = (((z_at - 2 * core) % zs ^ mask) + 2 * core) % zs
        pairs.append((at, 2 * partner + core))
    return lax.ppermute(value, "fsdp", pairs)


def by_core(value, axis, masks):
    count = lax.axis_size(axis)
    pairs = [
        (shard * count + at, shard * count + (at ^ masks[shard % 2]))
        for shard in range(lax.axis_size("fsdp"))
        for at in range(count)
    ]
    return lax.ppermute(value, ("fsdp", axis), pairs)


def swapped(value):
    return crossed(value, "fsdp", 1)


def on_device(weights, momentum, gradient, logit_max, layer_of):
    rank, cols = weights.shape[1:]
    fsdp = lax.axis_size("fsdp")
    layers = logit_max.shape[2]

    layer_match = jnp.arange(layers, dtype=jnp.int32)[None, :] == layer_of[:, None]
    peaks = jnp.max(jnp.where(layer_match[:, :, None], logit_max[0, 0][None], 0.0), axis=1)
    peaks = jnp.broadcast_to(peaks.reshape(1, BLOCK), (TAIL, BLOCK))

    keep, send = partial_gram(momentum, gradient)
    total = keep + swapped(send)
    total, peaks, late_momentum = lax.optimization_barrier((total, peaks, momentum))
    third, second, first = along_z(total, 3), along_z(total, 2), along_z(total, 1)
    total = (total + first) + (second + third)
    peaks = jnp.maximum(peaks, crossed(peaks, "ctx", 1))
    new_momentum = decayed(late_momentum, gradient)
    total, peaks, new_momentum = lax.optimization_barrier((total, peaks, new_momentum))
    total = total + along_z(total, 7)
    peaks = jnp.maximum(peaks, crossed(peaks, "ctx", 3))

    mine = jnp.concatenate([total, peaks], axis=0)
    halves = [mine] + [crossed(mine, "dp", mask) for mask in (1, 2, 3)]
    first, second, peaks = newton([piece for one in halves for piece in (one, swapped(one))], rank)
    update_scale = rms_factor * math.sqrt(max(rank, cols * fsdp))
    last = functools.partial(last_product, update_scale)
    near = tuple(by_core(piece, "ctx", (1, 3)) for piece in (first, second))
    new_weights = last((0, 0), weights, new_momentum, peaks, (first, second), None)
    near_first, new_weights = lax.optimization_barrier((near[0], new_weights))
    far = by_core(near_first, "ctx", (3, 1))
    cross = swapped(near[1]), swapped(near_first)
    new_weights = last((1, 3), weights, new_momentum, peaks, (near_first, near[1]), new_weights)
    far, new_weights = lax.optimization_barrier((far, new_weights))
    far = far, swapped(far)
    new_weights = last((3, 1), weights, new_momentum, peaks, cross, new_weights)
    new_weights = last((2, 2), weights, new_momentum, peaks, far, new_weights)
    return (new_weights, new_momentum)


def solution(mesh):
    in_specs = (
        P(None, None, "fsdp"),
        P(None, None, "fsdp"),
        P(None, None, "fsdp"),
        P("dp", "ctx", None, None),
        P(),
    )
    out_specs = (P(None, None, "fsdp"), P(None, None, "fsdp"))
    return jax.shard_map(
        on_device, mesh=mesh, in_specs=in_specs, out_specs=out_specs, check_vma=False
    )
```

```python
import functools
import math

import jax
import jax.numpy as jnp
from jax import lax
from jax.experimental import pallas as pl
from jax.experimental.pallas import tpu as pltpu
from jax.sharding import PartitionSpec as P

KNOPE = 128
VDIM = 128
ITERS = 5

quintic_a = 3.4445
quintic_b = -4.775
quintic_c = 2.0315
momentum_decay = 0.95
step_size = 0.1
clip_limit = 100.0
norm_eps = 1e-07
rms_factor = 0.2

BLOCK = 128
BLOCKS = 4
PART = 160
TAIL = 8
HALF = 640
END = 16
STRIP = 256
KEPT = [[(0, 0), (0, 1), (0, 2), (0, 3), (1, 1)], [(1, 2), (1, 3), (2, 2), (2, 3), (3, 3)]]


def decayed(momentum, gradient):
    return (momentum_decay * momentum.astype(jnp.float32) + gradient.astype(jnp.float32)).astype(jnp.bfloat16)


def aligned(index, to):
    return pl.multiple_of(index * to, to)


def partial_gram_kernel(momentum_ref, gradient_ref, keep_ref, send_ref, momentum, gradient, fresh, packed, arrived):
    matrix, dp_at, core = lax.axis_index("ctx"), lax.axis_index("dp"), lax.rem(lax.axis_index("fsdp"), 2)
    copies = []
    for at in (0, 2, 1):
        rows = pl.ds(aligned(lax.rem(dp_at + at, BLOCKS), BLOCK), BLOCK)
        pair = [
            pltpu.make_async_copy(source.at[matrix, rows], target.at[at], arrived.at[side, at])
            for side, (source, target) in enumerate(((momentum_ref, momentum), (gradient_ref, gradient)))
        ]
        for copy in pair:
            copy.start()
        copies.append((at, pair))
    for at, pair in copies:
        for copy in pair:
            copy.wait()
        fresh[at * BLOCK : (at + 1) * BLOCK, :] = decayed(momentum[at], gradient[at])

    def gram(left, right):
        return lax.dot_general(left, right, (((1,), (1,)), ((), ())), preferred_element_type=jnp.float32)

    early = dp_at < BLOCKS // 2
    far_rows = jnp.where(early, 0, 5)
    far_columns = jnp.where(early, 2, 0)
    packed[2 * BLOCK :, :] = gram(
        fresh[pl.ds(aligned(far_rows, BLOCK // 2), BLOCK // 2), :], fresh[pl.ds(aligned(far_columns, BLOCK), BLOCK), :]
    )
    packed[0:BLOCK, :] = gram(fresh[0:BLOCK, :], fresh[0:BLOCK, :])
    packed[BLOCK : 2 * BLOCK, :] = gram(fresh[0:BLOCK, :], fresh[BLOCK : 2 * BLOCK, :])
    keep_ref[...] = packed[pl.ds(aligned(core, PART), PART), :]
    send_ref[...] = packed[pl.ds(aligned(1 - core, PART), PART), :]


def partial_gram(momentum, gradient):
    rank, cols = momentum.shape[1:]
    shape = jax.ShapeDtypeStruct((PART, BLOCK), jnp.float32)
    blocks = pltpu.VMEM((3, BLOCK, cols), jnp.bfloat16)
    return pl.pallas_call(
        partial_gram_kernel,
        out_shape=(shape, shape),
        in_specs=[pl.BlockSpec(memory_space=pl.ANY)] * 2,
        out_specs=(pl.BlockSpec(memory_space=pltpu.VMEM),) * 2,
        scratch_shapes=[
            blocks,
            blocks,
            pltpu.VMEM((3 * BLOCK, cols), jnp.bfloat16),
            pltpu.VMEM((2 * PART, BLOCK), jnp.float32),
            pltpu.SemaphoreType.DMA((2, 3)),
        ],
        compiler_params=pltpu.CompilerParams(vmem_limit_bytes=62 * 2**20),
        cost_estimate=pl.CostEstimate(flops=4 * PART * BLOCK * cols, bytes_accessed=3 * rank * cols, transcendentals=0),
    )(momentum, gradient)


def split_in_two(value):
    high = value.astype(jnp.bfloat16)
    return high, (value - high.astype(jnp.float32)).astype(jnp.bfloat16)


def split_in_three(value):
    high = value.astype(jnp.bfloat16)
    rest = value - high.astype(jnp.float32)
    middle = rest.astype(jnp.bfloat16)
    return high, middle, (rest - middle.astype(jnp.float32)).astype(jnp.bfloat16)


def newton_kernel(*refs):
    parts, rest = [refs[2 * at : 2 * at + 2] for at in range(BLOCKS)], refs[2 * BLOCKS :]
    first_ref, second_ref, peaks_ref, packed, stacks, a_now, pair_a, pair_q, pair_b, pair_p, next_p = rest
    rank = a_now.shape[0]
    mid = rank // 2
    dp_at, core = lax.axis_index("dp"), lax.rem(lax.axis_index("fsdp"), 2)
    for turn, pair in enumerate(parts):
        for side, piece in enumerate(pair):
            half = core + side - 2 * core * side
            stacks[dp_at ^ turn, pl.ds(aligned(half, PART), PART), :] = piece[0:PART, :]
    peaks_ref[...] = functools.reduce(jnp.maximum, [pair[0][PART:, :] for pair in parts])

    def own_block(block):
        return stacks[block, 0:BLOCK, :]

    def beside(block):
        return stacks[block, BLOCK : 2 * BLOCK, :]

    eye = lax.broadcasted_iota(jnp.int32, (BLOCK, BLOCK), 0) == lax.broadcasted_iota(jnp.int32, (BLOCK, BLOCK), 1)
    diagonal = (own_block(0) + own_block(1)) + (own_block(2) + own_block(3))
    norm = jnp.sqrt(jnp.full((1, 1), jnp.sum(jnp.where(eye, diagonal, 0.0)), jnp.float32)) + norm_eps
    inverse = 1.0 / (norm * norm)

    def place(row, column, value):
        a_now[row * BLOCK : (row + 1) * BLOCK, column * BLOCK : (column + 1) * BLOCK] = value

    for block in range(BLOCKS):
        place(block, block, own_block(block) * inverse)
        after = (block + 1) % BLOCKS
        place(block, after, beside(block) * inverse)
        place(after, block, beside(block).T * inverse)
    for block in range(2):
        far_block = jnp.concatenate([stacks[block, 2 * BLOCK :, :], stacks[block + 2, 2 * BLOCK :, :]], axis=0) * inverse
        place(block, block + 2, far_block)
        place(block + 2, block, far_block.T)

    first, last = slice(0, mid), slice(mid, rank)
    rows_at = lax.broadcasted_iota(jnp.int32, (mid, rank), 0)
    columns_at = lax.broadcasted_iota(jnp.int32, (mid, rank), 1)
    shift = jnp.where(rows_at == columns_at, quintic_a, 0.0)
    dot = functools.partial(jnp.dot, preferred_element_type=jnp.float32)

    def keep(pair, rows, columns, value):
        pair[0, rows, columns], pair[1, rows, columns] = split_in_two(value)

    def product(left, right, rows, columns):
        high, low = left[0, rows, :], left[1, rows, :]
        return dot(high, right[0, :, columns]) + (dot(high, right[1, :, columns]) + dot(low, right[0, :, columns]))

    def whole_product(left, right, target, finish=None):
        for rows, columns in ((first, slice(0, rank)), (last, last)):
            value = product(left, right, rows, columns)
            if finish is not None:
                value = finish(value, rows, columns)
            keep(target, rows, columns, value)
            if rows == first:
                keep(target, last, first, value[:, mid:].T)

    def to_factor(square, rows, columns):
        return shift[:, 0 : square.shape[1]] + quintic_b * a_now[rows, columns] + quintic_c * square

    def store(value, rows, columns):
        a_now[rows, columns] = value
        return value

    for rows in (first, last):
        keep(pair_a, rows, slice(0, rank), a_now[rows, :])
    for iteration in range(ITERS - 1):
        whole_product(pair_a, pair_a, pair_q, to_factor)
        whole_product(pair_q, pair_a, pair_b)
        whole_product(pair_b, pair_q, pair_a, store)
        if iteration == 0:
            pair_p[...] = pair_q[...]
        else:
            whole_product(pair_p, pair_q, next_p)
            pair_p, next_p = next_p, pair_p
    whole_product(pair_a, pair_a, pair_q, to_factor)
    for rows, columns in ((first, slice(0, rank)), (last, last)):
        a_now[rows, columns] = product(pair_p, pair_q, rows, columns)
    for side, kept in enumerate(KEPT):
        for at, (row, column) in enumerate(kept):
            block = a_now[row * BLOCK : (row + 1) * BLOCK, column * BLOCK : (column + 1) * BLOCK]
            packed[side, at * BLOCK : (at + 1) * BLOCK, :] = block.astype(jnp.bfloat16)
    line = lax.broadcasted_iota(jnp.int32, (END, BLOCK), 0)
    spread = jnp.zeros((END, BLOCK), jnp.float32)
    for at, term in enumerate(split_in_three(norm)):
        spread = jnp.where(line == at, term.astype(jnp.float32), spread)
    for side in range(2):
        packed[side, HALF:, :] = spread.astype(jnp.bfloat16)
    first_ref[...] = packed[core]
    second_ref[...] = packed[1 - core]


def newton(parts, rank):
    whole = pl.BlockSpec(memory_space=pltpu.VMEM)
    pair = pltpu.VMEM((2, rank, rank), jnp.bfloat16)
    piece = jax.ShapeDtypeStruct((HALF + END, BLOCK), jnp.bfloat16)
    return pl.pallas_call(
        newton_kernel,
        out_shape=(piece, piece, jax.ShapeDtypeStruct((TAIL, BLOCK), jnp.float32)),
        in_specs=[whole] * len(parts),
        out_specs=(whole,) * 3,
        scratch_shapes=[
            pltpu.VMEM((2, HALF + END, BLOCK), jnp.bfloat16),
            pltpu.VMEM((BLOCKS, 2 * PART, BLOCK), jnp.float32),
            pltpu.VMEM((rank, rank), jnp.float32),
            pair,
            pair,
            pair,
            pair,
            pair,
        ],
        compiler_params=pltpu.CompilerParams(vmem_limit_bytes=40 * 2**20),
        cost_estimate=pl.CostEstimate(flops=17 * 6 * rank**3, bytes_accessed=6 * rank * rank, transcendentals=0),
    )(*parts)


def last_kernel(update_scale, masks, weights_ref, momentum_ref, peaks_ref, first_ref, second_ref, *refs):
    out_ref, packed, factors, fresh, left = refs[-5:]
    rank, cols = fresh.shape
    shard = lax.axis_index("fsdp")
    core = lax.rem(shard, 2)
    matrix = lax.axis_index("ctx") ^ (masks[0] + (masks[1] - masks[0]) * core)
    packed[core] = first_ref[...]
    packed[1 - core] = second_ref[...]
    for side, kept in enumerate(KEPT):
        for at, (row, column) in enumerate(kept):
            block = packed[side, at * BLOCK : (at + 1) * BLOCK, :]
            factors[row * BLOCK : (row + 1) * BLOCK, column * BLOCK : (column + 1) * BLOCK] = block
            if row != column:
                factors[column * BLOCK : (column + 1) * BLOCK, row * BLOCK : (row + 1) * BLOCK] = block.T
    end = first_ref[HALF:, :].astype(jnp.float32)
    inverse = 1.0 / ((end[0:1, 0:1] + end[1:2, 0:1]) + end[2:3, 0:1])
    heads = cols // (KNOPE + VDIM)
    column = lax.broadcasted_iota(jnp.int32, (1, cols), 1)
    lane = lax.broadcasted_iota(jnp.int32, (1, BLOCK), 1)
    column_peaks = jnp.full((1, cols), clip_limit, jnp.float32)
    for head in range(heads):
        place = matrix * (BLOCK // BLOCKS) + shard * heads + head
        peak = jnp.max(jnp.where(lane == place, peaks_ref[0:1, :], 0.0), axis=1, keepdims=True)
        first = head * (KNOPE + VDIM)
        column_peaks = jnp.where((column >= first) & (column < first + KNOPE), peak, column_peaks)
    scale = jnp.sqrt(jnp.minimum(1.0, clip_limit / column_peaks))
    start = (momentum_ref[matrix].astype(jnp.float32) * inverse).astype(jnp.bfloat16)
    stores = []
    for at in range(rank // STRIP):
        rows = slice(at * STRIP, (at + 1) * STRIP)
        orthogonal = jnp.dot(factors[rows, :], start, preferred_element_type=jnp.float32)
        value = weights_ref[matrix, rows, :].astype(jnp.float32) - step_size * (update_scale * orthogonal)
        fresh[rows, :] = (value * scale).astype(jnp.bfloat16)
        stores.append(pltpu.make_async_copy(fresh.at[rows], out_ref.at[matrix, rows], left.at[at]))
        stores[-1].start()
    for store in stores:
        store.wait()


def last_product(update_scale, masks, weights, momentum, peaks, pair, before):
    rank, cols = weights.shape[1:]
    whole, outside = pl.BlockSpec(memory_space=pltpu.VMEM), pl.BlockSpec(memory_space=pl.ANY)
    earlier = [] if before is None else [before]
    return pl.pallas_call(
        functools.partial(last_kernel, update_scale, masks),
        out_shape=jax.ShapeDtypeStruct(weights.shape, jnp.bfloat16),
        in_specs=[whole] * 5 + [outside] * len(earlier),
        out_specs=outside,
        scratch_shapes=[
            pltpu.VMEM((2, HALF + END, BLOCK), jnp.bfloat16),
            pltpu.VMEM((rank, rank), jnp.bfloat16),
            pltpu.VMEM((rank, cols), jnp.bfloat16),
            pltpu.SemaphoreType.DMA((rank // STRIP,)),
        ],
        input_output_aliases={5: 0} if earlier else {},
        compiler_params=pltpu.CompilerParams(vmem_limit_bytes=24 * 2**20),
        cost_estimate=pl.CostEstimate(flops=2 * rank * rank * cols, bytes_accessed=6 * rank * cols, transcendentals=0),
    )(weights, momentum, peaks, *pair, *earlier)


def fetch_kernel(source_ref, out_ref):
    out_ref[...] = source_ref[...]


def fetch(value):
    whole = pl.BlockSpec(memory_space=pltpu.VMEM)
    return pl.pallas_call(
        fetch_kernel,
        out_shape=jax.ShapeDtypeStruct(value.shape, value.dtype),
        in_specs=[whole],
        out_specs=whole,
        compiler_params=pltpu.CompilerParams(vmem_limit_bytes=8 * 2**20),
        cost_estimate=pl.CostEstimate(flops=0, bytes_accessed=8 * value.size, transcendentals=0),
    )(value)


def join_kernel(total_ref, arrived_ref, peaks_ref, peaks_arrived_ref, out_ref):
    out_ref[0:PART, :] = total_ref[...] + arrived_ref[...]
    out_ref[PART:, :] = jnp.maximum(peaks_ref[...], peaks_arrived_ref[...])


def join(*arrays):
    whole = pl.BlockSpec(memory_space=pltpu.VMEM)
    return pl.pallas_call(
        join_kernel,
        out_shape=jax.ShapeDtypeStruct((PART + TAIL, BLOCK), jnp.float32),
        in_specs=[whole] * 4,
        out_specs=whole,
        compiler_params=pltpu.CompilerParams(vmem_limit_bytes=8 * 2**20),
        cost_estimate=pl.CostEstimate(flops=PART * BLOCK, bytes_accessed=12 * PART * BLOCK, transcendentals=0),
    )(*arrays)


def crossed(value, axis, mask):
    return lax.ppermute(value, axis, [(at, at ^ mask) for at in range(lax.axis_size(axis))])


def along_z(value, mask):
    count = lax.axis_size("fsdp")
    zs = count // 2
    pairs = []
    for at in range(count):
        z_at, core = at // 2, at % 2
        partner = (((z_at - 2 * core) % zs ^ mask) + 2 * core) % zs
        pairs.append((at, 2 * partner + core))
    return lax.ppermute(value, "fsdp", pairs)


def by_core(value, axis, masks):
    count = lax.axis_size(axis)
    pairs = [
        (shard * count + at, shard * count + (at ^ masks[shard % 2]))
        for shard in range(lax.axis_size("fsdp"))
        for at in range(count)
    ]
    return lax.ppermute(value, ("fsdp", axis), pairs)


def swapped(value):
    return crossed(value, "fsdp", 1)


def on_device(weights, momentum, gradient, logit_max, layer_of):
    rank, cols = weights.shape[1:]
    fsdp = lax.axis_size("fsdp")
    layers = logit_max.shape[2]

    layer_match = jnp.arange(layers, dtype=jnp.int32)[None, :] == layer_of[:, None]
    peaks = jnp.max(jnp.where(layer_match[:, :, None], logit_max[0, 0][None], 0.0), axis=1)
    peaks = jnp.broadcast_to(peaks.reshape(1, BLOCK), (TAIL, BLOCK))

    keep, send = partial_gram(momentum, gradient)
    total = fetch(keep) + swapped(send)
    total, peaks, late_momentum = lax.optimization_barrier((total, peaks, momentum))
    third, second, first = along_z(total, 3), along_z(total, 2), along_z(total, 1)
    total = (total + first) + (second + third)
    peaks = jnp.maximum(peaks, crossed(peaks, "ctx", 1))
    new_momentum = decayed(late_momentum, gradient)
    total, peaks, new_momentum = lax.optimization_barrier((total, peaks, new_momentum))
    mine = join(total, along_z(total, 7), peaks, crossed(peaks, "ctx", 3))
    halves = [mine] + [crossed(mine, "dp", mask) for mask in (1, 2, 3)]
    first, second, peaks = newton([piece for one in halves for piece in (one, swapped(one))], rank)
    update_scale = rms_factor * math.sqrt(max(rank, cols * fsdp))
    last = functools.partial(last_product, update_scale)
    near = tuple(by_core(piece, "ctx", (1, 3)) for piece in (first, second))
    new_weights = last((0, 0), weights, new_momentum, peaks, (first, second), None)
    near_first, new_weights = lax.optimization_barrier((near[0], new_weights))
    far = by_core(near_first, "ctx", (3, 1))
    cross = swapped(near[1]), swapped(near_first)
    new_weights = last((1, 3), weights, new_momentum, peaks, (near_first, near[1]), new_weights)
    far, new_weights = lax.optimization_barrier((far, new_weights))
    far = far, swapped(far)
    new_weights = last((3, 1), weights, new_momentum, peaks, cross, new_weights)
    new_weights = last((2, 2), weights, new_momentum, peaks, far, new_weights)
    return (new_weights, new_momentum)


def solution(mesh):
    in_specs = (
        P(None, None, "fsdp"),
        P(None, None, "fsdp"),
        P(None, None, "fsdp"),
        P("dp", "ctx", None, None),
        P(),
    )
    out_specs = (P(None, None, "fsdp"), P(None, None, "fsdp"))
    return jax.shard_map(
        on_device, mesh=mesh, in_specs=in_specs, out_specs=out_specs, check_vma=False
    )
```

```python
import functools
import math

import jax
import jax.numpy as jnp
from jax import lax
from jax.experimental import pallas as pl
from jax.experimental.pallas import tpu as pltpu
from jax.sharding import PartitionSpec as P

KNOPE = 128
VDIM = 128
ITERS = 5

quintic_a = 3.4445
quintic_b = -4.775
quintic_c = 2.0315
momentum_decay = 0.95
step_size = 0.1
clip_limit = 100.0
norm_eps = 1e-07
rms_factor = 0.2

BLOCK = 128
BLOCKS = 4
HALF_BLOCK = 64
PART = 144
TAIL = 8
HALF = 640
END = 16
STRIP = 256
KEPT = [[(0, 0), (0, 1), (0, 2), (0, 3), (1, 1)], [(1, 2), (1, 3), (2, 2), (2, 3), (3, 3)]]


def decayed(momentum, gradient):
    return (momentum_decay * momentum.astype(jnp.float32) + gradient.astype(jnp.float32)).astype(jnp.bfloat16)


def aligned(index, to):
    return pl.multiple_of(index * to, to)


def partial_gram_kernel(momentum_ref, gradient_ref, keep_ref, send_ref, momentum, gradient, fresh, packed, arrived):
    matrix, dp_at, core = lax.axis_index("ctx"), lax.axis_index("dp"), lax.rem(lax.axis_index("fsdp"), 2)
    copies = []
    for at in (0, 2, 1):
        rows = pl.ds(aligned(lax.rem(dp_at + at, BLOCKS), BLOCK), BLOCK)
        pair = [
            pltpu.make_async_copy(source.at[matrix, rows], target.at[at], arrived.at[side, at])
            for side, (source, target) in enumerate(((momentum_ref, momentum), (gradient_ref, gradient)))
        ]
        for copy in pair:
            copy.start()
        copies.append((at, pair))
    for at, pair in copies:
        for copy in pair:
            copy.wait()
        fresh[at * BLOCK : (at + 1) * BLOCK, :] = decayed(momentum[at], gradient[at])

    def gram(left, right):
        return lax.dot_general(left, right, (((1,), (1,)), ((), ())), preferred_element_type=jnp.float32)

    early = dp_at < BLOCKS // 2
    far_rows = jnp.where(early, 0, 5)
    far_columns = jnp.where(early, 2, 0)
    packed[7 * HALF_BLOCK // 2 :, :] = gram(
        fresh[pl.ds(aligned(far_rows, BLOCK // 2), BLOCK // 2), :], fresh[pl.ds(aligned(far_columns, BLOCK), BLOCK), :]
    )
    own = gram(fresh[0:BLOCK, :], fresh[0:BLOCK, :])
    packed[0:HALF_BLOCK, :] = own[0:HALF_BLOCK, :]
    quarter = HALF_BLOCK // 2
    left_half = lax.broadcasted_iota(jnp.int32, (quarter, BLOCK), 1) < HALF_BLOCK
    third, fourth = own[2 * quarter : 3 * quarter, :], own[3 * quarter :, :]
    packed[HALF_BLOCK : 3 * quarter, :] = jnp.where(left_half, pltpu.roll(third, HALF_BLOCK, 1), fourth)
    packed[3 * quarter : 3 * quarter + BLOCK, :] = gram(fresh[0:BLOCK, :], fresh[BLOCK : 2 * BLOCK, :])
    keep_ref[...] = packed[pl.ds(aligned(core, PART), PART), :]
    send_ref[...] = packed[pl.ds(aligned(1 - core, PART), PART), :]


def partial_gram(momentum, gradient):
    rank, cols = momentum.shape[1:]
    shape = jax.ShapeDtypeStruct((PART, BLOCK), jnp.float32)
    blocks = pltpu.VMEM((3, BLOCK, cols), jnp.bfloat16)
    return pl.pallas_call(
        partial_gram_kernel,
        out_shape=(shape, shape),
        in_specs=[pl.BlockSpec(memory_space=pl.ANY)] * 2,
        out_specs=(pl.BlockSpec(memory_space=pltpu.VMEM),) * 2,
        scratch_shapes=[
            blocks,
            blocks,
            pltpu.VMEM((3 * BLOCK, cols), jnp.bfloat16),
            pltpu.VMEM((2 * PART, BLOCK), jnp.float32),
            pltpu.SemaphoreType.DMA((2, 3)),
        ],
        compiler_params=pltpu.CompilerParams(vmem_limit_bytes=62 * 2**20),
        cost_estimate=pl.CostEstimate(flops=4 * PART * BLOCK * cols, bytes_accessed=3 * rank * cols, transcendentals=0),
    )(momentum, gradient)


def split_in_two(value):
    high = value.astype(jnp.bfloat16)
    return high, (value - high.astype(jnp.float32)).astype(jnp.bfloat16)


def split_in_three(value):
    high = value.astype(jnp.bfloat16)
    rest = value - high.astype(jnp.float32)
    middle = rest.astype(jnp.bfloat16)
    return high, middle, (rest - middle.astype(jnp.float32)).astype(jnp.bfloat16)


def newton_kernel(*refs):
    parts, rest = [refs[2 * at : 2 * at + 2] for at in range(BLOCKS)], refs[2 * BLOCKS :]
    first_ref, second_ref, peaks_ref, packed, stacks, a_now, pair_a, pair_q, pair_b, pair_p, next_p = rest
    rank = a_now.shape[0]
    mid = rank // 2
    dp_at, core = lax.axis_index("dp"), lax.rem(lax.axis_index("fsdp"), 2)
    for turn, pair in enumerate(parts):
        for side, piece in enumerate(pair):
            half = core + side - 2 * core * side
            stacks[dp_at ^ turn, pl.ds(aligned(half, PART), PART), :] = piece[0:PART, :]
    peaks_ref[...] = functools.reduce(jnp.maximum, [pair[0][PART:, :] for pair in parts])

    quarter = HALF_BLOCK // 2
    rows_in = lax.broadcasted_iota(jnp.int32, (BLOCK, BLOCK), 0)
    columns_in = lax.broadcasted_iota(jnp.int32, (BLOCK, BLOCK), 1)
    missing = (rows_in >= HALF_BLOCK) & (columns_in < HALF_BLOCK)

    def own_block(block):
        low = stacks[block, HALF_BLOCK : 3 * quarter, :]
        return jnp.concatenate([stacks[block, 0:HALF_BLOCK, :], pltpu.roll(low, HALF_BLOCK, 1), low], axis=0)

    def beside(block):
        return stacks[block, 3 * quarter : 3 * quarter + BLOCK, :]

    def far(block):
        return stacks[block, 3 * quarter + BLOCK :, :]

    owns = [own_block(block) for block in range(BLOCKS)]
    diagonal = (owns[0] + owns[1]) + (owns[2] + owns[3])
    trace = jnp.sum(jnp.where(rows_in == columns_in, diagonal, 0.0))
    norm = jnp.sqrt(jnp.full((1, 1), trace, jnp.float32)) + norm_eps
    inverse = 1.0 / (norm * norm)

    def place(row, column, value):
        a_now[row * BLOCK : (row + 1) * BLOCK, column * BLOCK : (column + 1) * BLOCK] = value

    for block in range(BLOCKS):
        place(block, block, jnp.where(missing, owns[block].T, owns[block]))
        after = (block + 1) % BLOCKS
        place(block, after, beside(block))
        place(after, block, beside(block).T)
    for block in range(2):
        far_block = jnp.concatenate([far(block), far(block + 2)], axis=0)
        place(block, block + 2, far_block)
        place(block + 2, block, far_block.T)

    first, last = slice(0, mid), slice(mid, rank)
    rows_at = lax.broadcasted_iota(jnp.int32, (mid, rank), 0)
    columns_at = lax.broadcasted_iota(jnp.int32, (mid, rank), 1)
    shift = jnp.where(rows_at == columns_at, quintic_a, 0.0)
    dot = functools.partial(jnp.dot, preferred_element_type=jnp.float32)

    def keep(pair, rows, columns, value):
        strip = rows.start // mid
        pair[strip, 0, :, columns], pair[strip, 1, :, columns] = split_in_two(value)

    def product(left, right, rows, columns):
        strip = rows.start // mid
        high, low = [right[:, term, :, columns].reshape(rank, -1) for term in range(2)]
        both = dot(left[strip].reshape(rank, rank), high)
        return both[0:mid] + (both[mid:] + dot(left[strip, 0], low))

    def whole_product(left, right, target, finish=None):
        for rows, columns in ((first, slice(0, rank)), (last, last)):
            value = product(left, right, rows, columns)
            if finish is not None:
                value = finish(value, rows, columns)
            keep(target, rows, columns, value)
            if rows == first:
                keep(target, last, first, value[:, mid:].T)

    def to_factor(square, rows, columns):
        return shift[:, 0 : square.shape[1]] + quintic_b * a_now[rows, columns] + quintic_c * square

    def to_first_factor(square, rows, columns):
        return shift[:, 0 : square.shape[1]] + (quintic_b * inverse) * a_now[rows, columns] + (quintic_c * inverse) * (square * inverse)

    def scaled(value, rows, columns):
        return value * inverse

    def store(value, rows, columns):
        a_now[rows, columns] = value
        return value

    for rows in (first, last):
        keep(pair_a, rows, slice(0, rank), a_now[rows, :])
    for iteration in range(ITERS - 1):
        whole_product(pair_a, pair_a, pair_q, to_factor if iteration else to_first_factor)
        whole_product(pair_q, pair_a, pair_b, None if iteration else scaled)
        whole_product(pair_b, pair_q, pair_a, store)
        if iteration == 0:
            pair_p[...] = pair_q[...]
        else:
            whole_product(pair_p, pair_q, next_p)
            pair_p, next_p = next_p, pair_p
    whole_product(pair_a, pair_a, pair_q, to_factor)
    for rows, columns in ((first, slice(0, rank)), (last, last)):
        a_now[rows, columns] = product(pair_p, pair_q, rows, columns)
    for side, kept in enumerate(KEPT):
        for at, (row, column) in enumerate(kept):
            block = a_now[row * BLOCK : (row + 1) * BLOCK, column * BLOCK : (column + 1) * BLOCK]
            packed[side, at * BLOCK : (at + 1) * BLOCK, :] = block.astype(jnp.bfloat16)
    line = lax.broadcasted_iota(jnp.int32, (END, BLOCK), 0)
    spread = jnp.zeros((END, BLOCK), jnp.float32)
    for at, term in enumerate(split_in_three(norm)):
        spread = jnp.where(line == at, term.astype(jnp.float32), spread)
    for side in range(2):
        packed[side, HALF:, :] = spread.astype(jnp.bfloat16)
    first_ref[...] = packed[core]
    second_ref[...] = packed[1 - core]


def newton(parts, rank):
    whole = pl.BlockSpec(memory_space=pltpu.VMEM)
    pair = pltpu.VMEM((2, 2, rank // 2, rank), jnp.bfloat16)
    piece = jax.ShapeDtypeStruct((HALF + END, BLOCK), jnp.bfloat16)
    return pl.pallas_call(
        newton_kernel,
        out_shape=(piece, piece, jax.ShapeDtypeStruct((TAIL, BLOCK), jnp.float32)),
        in_specs=[whole] * len(parts),
        out_specs=(whole,) * 3,
        scratch_shapes=[
            pltpu.VMEM((2, HALF + END, BLOCK), jnp.bfloat16),
            pltpu.VMEM((BLOCKS, 2 * PART, BLOCK), jnp.float32),
            pltpu.VMEM((rank, rank), jnp.float32),
            pair,
            pair,
            pair,
            pair,
            pair,
        ],
        compiler_params=pltpu.CompilerParams(vmem_limit_bytes=40 * 2**20),
        cost_estimate=pl.CostEstimate(flops=17 * 6 * rank**3, bytes_accessed=6 * rank * rank, transcendentals=0),
    )(*parts)


def last_kernel(update_scale, masks, weights_ref, momentum_ref, peaks_ref, first_ref, second_ref, *refs):
    out_ref, packed, factors, fresh, left = refs[-5:]
    rank, cols = fresh.shape
    shard = lax.axis_index("fsdp")
    core = lax.rem(shard, 2)
    matrix = lax.axis_index("ctx") ^ (masks[0] + (masks[1] - masks[0]) * core)
    packed[core] = first_ref[...]
    packed[1 - core] = second_ref[...]
    for side, kept in enumerate(KEPT):
        for at, (row, column) in enumerate(kept):
            block = packed[side, at * BLOCK : (at + 1) * BLOCK, :]
            factors[row * BLOCK : (row + 1) * BLOCK, column * BLOCK : (column + 1) * BLOCK] = block
            if row != column:
                factors[column * BLOCK : (column + 1) * BLOCK, row * BLOCK : (row + 1) * BLOCK] = block.T
    end = first_ref[HALF:, :].astype(jnp.float32)
    inverse = 1.0 / ((end[0:1, 0:1] + end[1:2, 0:1]) + end[2:3, 0:1])
    heads = cols // (KNOPE + VDIM)
    column = lax.broadcasted_iota(jnp.int32, (1, cols), 1)
    lane = lax.broadcasted_iota(jnp.int32, (1, BLOCK), 1)
    column_peaks = jnp.full((1, cols), clip_limit, jnp.float32)
    for head in range(heads):
        place = matrix * (BLOCK // BLOCKS) + shard * heads + head
        peak = jnp.max(jnp.where(lane == place, peaks_ref[0:1, :], 0.0), axis=1, keepdims=True)
        first = head * (KNOPE + VDIM)
        column_peaks = jnp.where((column >= first) & (column < first + KNOPE), peak, column_peaks)
    scale = jnp.sqrt(jnp.minimum(1.0, clip_limit / column_peaks))
    start = (momentum_ref[matrix].astype(jnp.float32) * inverse).astype(jnp.bfloat16)
    stores = []
    for at in range(rank // STRIP):
        rows = slice(at * STRIP, (at + 1) * STRIP)
        orthogonal = jnp.dot(factors[rows, :], start, preferred_element_type=jnp.float32)
        value = weights_ref[matrix, rows, :].astype(jnp.float32) - step_size * (update_scale * orthogonal)
        fresh[rows, :] = (value * scale).astype(jnp.bfloat16)
        stores.append(pltpu.make_async_copy(fresh.at[rows], out_ref.at[matrix, rows], left.at[at]))
        stores[-1].start()
    for store in stores:
        store.wait()


def last_product(update_scale, masks, weights, momentum, peaks, pair, before):
    rank, cols = weights.shape[1:]
    whole, outside = pl.BlockSpec(memory_space=pltpu.VMEM), pl.BlockSpec(memory_space=pl.ANY)
    earlier = [] if before is None else [before]
    return pl.pallas_call(
        functools.partial(last_kernel, update_scale, masks),
        out_shape=jax.ShapeDtypeStruct(weights.shape, jnp.bfloat16),
        in_specs=[whole] * 5 + [outside] * len(earlier),
        out_specs=outside,
        scratch_shapes=[
            pltpu.VMEM((2, HALF + END, BLOCK), jnp.bfloat16),
            pltpu.VMEM((rank, rank), jnp.bfloat16),
            pltpu.VMEM((rank, cols), jnp.bfloat16),
            pltpu.SemaphoreType.DMA((rank // STRIP,)),
        ],
        input_output_aliases={5: 0} if earlier else {},
        compiler_params=pltpu.CompilerParams(vmem_limit_bytes=24 * 2**20),
        cost_estimate=pl.CostEstimate(flops=2 * rank * rank * cols, bytes_accessed=6 * rank * cols, transcendentals=0),
    )(weights, momentum, peaks, *pair, *earlier)


def fetch_kernel(source_ref, out_ref):
    out_ref[...] = source_ref[...]


def fetch(value):
    whole = pl.BlockSpec(memory_space=pltpu.VMEM)
    return pl.pallas_call(
        fetch_kernel,
        out_shape=jax.ShapeDtypeStruct(value.shape, value.dtype),
        in_specs=[whole],
        out_specs=whole,
        compiler_params=pltpu.CompilerParams(vmem_limit_bytes=8 * 2**20),
        cost_estimate=pl.CostEstimate(flops=0, bytes_accessed=8 * value.size, transcendentals=0),
    )(value)


def join_kernel(total_ref, arrived_ref, peaks_ref, peaks_arrived_ref, out_ref):
    out_ref[0:PART, :] = total_ref[...] + arrived_ref[...]
    out_ref[PART:, :] = jnp.maximum(peaks_ref[...], peaks_arrived_ref[...])


def join(*arrays):
    whole = pl.BlockSpec(memory_space=pltpu.VMEM)
    return pl.pallas_call(
        join_kernel,
        out_shape=jax.ShapeDtypeStruct((PART + TAIL, BLOCK), jnp.float32),
        in_specs=[whole] * 4,
        out_specs=whole,
        compiler_params=pltpu.CompilerParams(vmem_limit_bytes=8 * 2**20),
        cost_estimate=pl.CostEstimate(flops=PART * BLOCK, bytes_accessed=12 * PART * BLOCK, transcendentals=0),
    )(*arrays)


def crossed(value, axis, mask):
    return lax.ppermute(value, axis, [(at, at ^ mask) for at in range(lax.axis_size(axis))])


def along_z(value, mask):
    count = lax.axis_size("fsdp")
    zs = count // 2
    pairs = []
    for at in range(count):
        z_at, core = at // 2, at % 2
        partner = (((z_at - 2 * core) % zs ^ mask) + 2 * core) % zs
        pairs.append((at, 2 * partner + core))
    return lax.ppermute(value, "fsdp", pairs)


def by_core(value, axis, masks):
    count = lax.axis_size(axis)
    pairs = [
        (shard * count + at, shard * count + (at ^ masks[shard % 2]))
        for shard in range(lax.axis_size("fsdp"))
        for at in range(count)
    ]
    return lax.ppermute(value, ("fsdp", axis), pairs)


def swapped(value):
    return crossed(value, "fsdp", 1)


def on_device(weights, momentum, gradient, logit_max, layer_of):
    rank, cols = weights.shape[1:]
    fsdp = lax.axis_size("fsdp")
    layers = logit_max.shape[2]

    layer_match = jnp.arange(layers, dtype=jnp.int32)[None, :] == layer_of[:, None]
    peaks = jnp.max(jnp.where(layer_match[:, :, None], logit_max[0, 0][None], 0.0), axis=1)
    peaks = jnp.broadcast_to(peaks.reshape(1, BLOCK), (TAIL, BLOCK))

    keep, send = partial_gram(momentum, gradient)
    total = fetch(keep) + swapped(send)
    total, peaks = lax.optimization_barrier((total, peaks))
    third, second, first = along_z(total, 3), along_z(total, 2), along_z(total, 1)
    total = (total + first) + (second + third)
    peaks = jnp.maximum(peaks, crossed(peaks, "ctx", 1))
    total, peaks = lax.optimization_barrier((total, peaks))
    mine = join(total, along_z(total, 7), peaks, crossed(peaks, "ctx", 3))
    halves = [mine] + [crossed(mine, "dp", mask) for mask in (1, 2, 3)]
    first, second, peaks = newton([piece for one in halves for piece in (one, swapped(one))], rank)
    update_scale = rms_factor * math.sqrt(max(rank, cols * fsdp))
    last = functools.partial(last_product, update_scale)
    peaks, late_momentum = lax.optimization_barrier((peaks, momentum))
    new_momentum = decayed(late_momentum, gradient)
    near = tuple(by_core(piece, "ctx", (1, 3)) for piece in (first, second))
    new_weights = last((0, 0), weights, new_momentum, peaks, (first, second), None)
    near_first, new_weights = lax.optimization_barrier((near[0], new_weights))
    far = by_core(near_first, "ctx", (3, 1))
    cross = swapped(near[1]), swapped(near_first)
    new_weights = last((1, 3), weights, new_momentum, peaks, (near_first, near[1]), new_weights)
    far, new_weights = lax.optimization_barrier((far, new_weights))
    far = far, swapped(far)
    new_weights = last((3, 1), weights, new_momentum, peaks, cross, new_weights)
    new_weights = last((2, 2), weights, new_momentum, peaks, far, new_weights)
    return (new_weights, new_momentum)


def solution(mesh):
    in_specs = (
        P(None, None, "fsdp"),
        P(None, None, "fsdp"),
        P(None, None, "fsdp"),
        P("dp", "ctx", None, None),
        P(),
    )
    out_specs = (P(None, None, "fsdp"), P(None, None, "fsdp"))
    return jax.shard_map(
        on_device, mesh=mesh, in_specs=in_specs, out_specs=out_specs, check_vma=False
    )
```

```python
import functools
import math

import jax
import jax.numpy as jnp
from jax import lax
from jax.experimental import pallas as pl
from jax.experimental.pallas import tpu as pltpu
from jax.sharding import PartitionSpec as P

KNOPE = 128
VDIM = 128
ITERS = 5

quintic_a = 3.4445
quintic_b = -4.775
quintic_c = 2.0315
momentum_decay = 0.95
step_size = 0.1
clip_limit = 100.0
norm_eps = 1e-07
rms_factor = 0.2

BLOCK = 128
BLOCKS = 4
HALF_BLOCK = 64
PART = 144
TAIL = 8
HALF = 640
END = 16
STRIP = 256
KEPT = [[(0, 0), (0, 1), (0, 2), (0, 3), (1, 1)], [(1, 2), (1, 3), (2, 2), (2, 3), (3, 3)]]


def decayed(momentum, gradient):
    return (momentum_decay * momentum.astype(jnp.float32) + gradient.astype(jnp.float32)).astype(jnp.bfloat16)


def aligned(index, to):
    return pl.multiple_of(index * to, to)


def partial_gram_kernel(momentum_ref, gradient_ref, keep_ref, send_ref, momentum, gradient, fresh, packed, arrived):
    matrix, dp_at, core = lax.axis_index("ctx"), lax.axis_index("dp"), lax.rem(lax.axis_index("fsdp"), 2)
    copies = []
    for at in (0, 2, 1):
        rows = pl.ds(aligned(lax.rem(dp_at + at, BLOCKS), BLOCK), BLOCK)
        pair = [
            pltpu.make_async_copy(source.at[matrix, rows], target.at[at], arrived.at[side, at])
            for side, (source, target) in enumerate(((momentum_ref, momentum), (gradient_ref, gradient)))
        ]
        for copy in pair:
            copy.start()
        copies.append((at, pair))
    for at, pair in copies:
        for copy in pair:
            copy.wait()
        fresh[at * BLOCK : (at + 1) * BLOCK, :] = decayed(momentum[at], gradient[at])

    def gram(left, right):
        return lax.dot_general(left, right, (((1,), (1,)), ((), ())), preferred_element_type=jnp.float32)

    early = dp_at < BLOCKS // 2
    far_rows = jnp.where(early, 0, 5)
    far_columns = jnp.where(early, 2, 0)
    packed[7 * HALF_BLOCK // 2 :, :] = gram(
        fresh[pl.ds(aligned(far_rows, BLOCK // 2), BLOCK // 2), :], fresh[pl.ds(aligned(far_columns, BLOCK), BLOCK), :]
    )
    own = gram(fresh[0:BLOCK, :], fresh[0:BLOCK, :])
    packed[0:HALF_BLOCK, :] = own[0:HALF_BLOCK, :]
    quarter = HALF_BLOCK // 2
    left_half = lax.broadcasted_iota(jnp.int32, (quarter, BLOCK), 1) < HALF_BLOCK
    third, fourth = own[2 * quarter : 3 * quarter, :], own[3 * quarter :, :]
    packed[HALF_BLOCK : 3 * quarter, :] = jnp.where(left_half, pltpu.roll(third, HALF_BLOCK, 1), fourth)
    packed[3 * quarter : 3 * quarter + BLOCK, :] = gram(fresh[0:BLOCK, :], fresh[BLOCK : 2 * BLOCK, :])
    keep_ref[...] = packed[pl.ds(aligned(core, PART), PART), :]
    send_ref[...] = packed[pl.ds(aligned(1 - core, PART), PART), :]


def partial_gram(momentum, gradient):
    rank, cols = momentum.shape[1:]
    shape = jax.ShapeDtypeStruct((PART, BLOCK), jnp.float32)
    blocks = pltpu.VMEM((3, BLOCK, cols), jnp.bfloat16)
    return pl.pallas_call(
        partial_gram_kernel,
        out_shape=(shape, shape),
        in_specs=[pl.BlockSpec(memory_space=pl.ANY)] * 2,
        out_specs=(pl.BlockSpec(memory_space=pltpu.VMEM),) * 2,
        scratch_shapes=[
            blocks,
            blocks,
            pltpu.VMEM((3 * BLOCK, cols), jnp.bfloat16),
            pltpu.VMEM((2 * PART, BLOCK), jnp.float32),
            pltpu.SemaphoreType.DMA((2, 3)),
        ],
        compiler_params=pltpu.CompilerParams(vmem_limit_bytes=53 * 2**20),
        cost_estimate=pl.CostEstimate(flops=4 * PART * BLOCK * cols, bytes_accessed=3 * rank * cols, transcendentals=0),
    )(momentum, gradient)


def split_in_two(value):
    high = value.astype(jnp.bfloat16)
    return high, (value - high.astype(jnp.float32)).astype(jnp.bfloat16)


def split_in_three(value):
    high = value.astype(jnp.bfloat16)
    rest = value - high.astype(jnp.float32)
    middle = rest.astype(jnp.bfloat16)
    return high, middle, (rest - middle.astype(jnp.float32)).astype(jnp.bfloat16)


def newton_kernel(*refs):
    parts, rest = [refs[2 * at : 2 * at + 2] for at in range(BLOCKS)], refs[2 * BLOCKS :]
    first_ref, second_ref, peaks_ref, packed, stacks, a_now, pair_a, pair_q, pair_b, pair_p, next_p = rest
    rank = a_now.shape[0]
    mid = rank // 2
    dp_at, core = lax.axis_index("dp"), lax.rem(lax.axis_index("fsdp"), 2)
    for turn, pair in enumerate(parts):
        for side, piece in enumerate(pair):
            half = core + side - 2 * core * side
            stacks[dp_at ^ turn, pl.ds(aligned(half, PART), PART), :] = piece[0:PART, :]
    peaks_ref[...] = functools.reduce(jnp.maximum, [pair[0][PART:, :] for pair in parts])

    quarter = HALF_BLOCK // 2
    rows_in = lax.broadcasted_iota(jnp.int32, (BLOCK, BLOCK), 0)
    columns_in = lax.broadcasted_iota(jnp.int32, (BLOCK, BLOCK), 1)
    missing = (rows_in >= HALF_BLOCK) & (columns_in < HALF_BLOCK)

    def own_block(block):
        low = stacks[block, HALF_BLOCK : 3 * quarter, :]
        return jnp.concatenate([stacks[block, 0:HALF_BLOCK, :], pltpu.roll(low, HALF_BLOCK, 1), low], axis=0)

    def beside(block):
        return stacks[block, 3 * quarter : 3 * quarter + BLOCK, :]

    def far(block):
        return stacks[block, 3 * quarter + BLOCK :, :]

    owns = [own_block(block) for block in range(BLOCKS)]
    diagonal = (owns[0] + owns[1]) + (owns[2] + owns[3])
    trace = jnp.sum(jnp.where(rows_in == columns_in, diagonal, 0.0))
    norm = jnp.sqrt(jnp.full((1, 1), trace, jnp.float32)) + norm_eps
    inverse = 1.0 / (norm * norm)

    def place(row, column, value):
        a_now[row * BLOCK : (row + 1) * BLOCK, column * BLOCK : (column + 1) * BLOCK] = value

    for block in range(BLOCKS):
        place(block, block, jnp.where(missing, owns[block].T, owns[block]))
        after = (block + 1) % BLOCKS
        place(block, after, beside(block))
        place(after, block, beside(block).T)
    for block in range(2):
        far_block = jnp.concatenate([far(block), far(block + 2)], axis=0)
        place(block, block + 2, far_block)
        place(block + 2, block, far_block.T)

    first, last = slice(0, mid), slice(mid, rank)
    rows_at = lax.broadcasted_iota(jnp.int32, (mid, rank), 0)
    columns_at = lax.broadcasted_iota(jnp.int32, (mid, rank), 1)
    shift = jnp.where(rows_at == columns_at, quintic_a, 0.0)
    dot = functools.partial(jnp.dot, preferred_element_type=jnp.float32)

    def keep(pair, rows, columns, value):
        strip = rows.start // mid
        pair[strip, 0, :, columns], pair[strip, 1, :, columns] = split_in_two(value)

    def product(left, right, rows, columns):
        strip = rows.start // mid
        high, low = [right[:, term, :, columns].reshape(rank, -1) for term in range(2)]
        both = dot(left[strip].reshape(rank, rank), high)
        return both[0:mid] + (both[mid:] + dot(left[strip, 0], low))

    def whole_product(left, right, target, finish=None):
        for rows, columns in ((first, slice(0, rank)), (last, last)):
            value = product(left, right, rows, columns)
            if finish is not None:
                value = finish(value, rows, columns)
            keep(target, rows, columns, value)
            if rows == first:
                keep(target, last, first, value[:, mid:].T)

    def to_factor(square, rows, columns):
        return shift[:, 0 : square.shape[1]] + quintic_b * a_now[rows, columns] + quintic_c * square

    def to_first_factor(square, rows, columns):
        return shift[:, 0 : square.shape[1]] + (quintic_b * inverse) * a_now[rows, columns] + (quintic_c * inverse) * (square * inverse)

    def scaled(value, rows, columns):
        return value * inverse

    def store(value, rows, columns):
        a_now[rows, columns] = value
        return value

    for rows in (first, last):
        keep(pair_a, rows, slice(0, rank), a_now[rows, :])
    for iteration in range(ITERS - 1):
        whole_product(pair_a, pair_a, pair_q, to_factor if iteration else to_first_factor)
        whole_product(pair_q, pair_a, pair_b, None if iteration else scaled)
        whole_product(pair_b, pair_q, pair_a, store)
        if iteration == 0:
            pair_p[...] = pair_q[...]
        else:
            whole_product(pair_p, pair_q, next_p)
            pair_p, next_p = next_p, pair_p
    whole_product(pair_a, pair_a, pair_q, to_factor)
    for rows, columns in ((first, slice(0, rank)), (last, last)):
        a_now[rows, columns] = product(pair_p, pair_q, rows, columns)
    for side, kept in enumerate(KEPT):
        for at, (row, column) in enumerate(kept):
            block = a_now[row * BLOCK : (row + 1) * BLOCK, column * BLOCK : (column + 1) * BLOCK]
            packed[side, at * BLOCK : (at + 1) * BLOCK, :] = block.astype(jnp.bfloat16)
    line = lax.broadcasted_iota(jnp.int32, (END, BLOCK), 0)
    spread = jnp.zeros((END, BLOCK), jnp.float32)
    for at, term in enumerate(split_in_three(norm)):
        spread = jnp.where(line == at, term.astype(jnp.float32), spread)
    for side in range(2):
        packed[side, HALF:, :] = spread.astype(jnp.bfloat16)
    first_ref[...] = packed[core]
    second_ref[...] = packed[1 - core]


def newton(parts, rank):
    whole = pl.BlockSpec(memory_space=pltpu.VMEM)
    pair = pltpu.VMEM((2, 2, rank // 2, rank), jnp.bfloat16)
    piece = jax.ShapeDtypeStruct((HALF + END, BLOCK), jnp.bfloat16)
    return pl.pallas_call(
        newton_kernel,
        out_shape=(piece, piece, jax.ShapeDtypeStruct((TAIL, BLOCK), jnp.float32)),
        in_specs=[whole] * len(parts),
        out_specs=(whole,) * 3,
        scratch_shapes=[
            pltpu.VMEM((2, HALF + END, BLOCK), jnp.bfloat16),
            pltpu.VMEM((BLOCKS, 2 * PART, BLOCK), jnp.float32),
            pltpu.VMEM((rank, rank), jnp.float32),
            pair,
            pair,
            pair,
            pair,
            pair,
        ],
        compiler_params=pltpu.CompilerParams(vmem_limit_bytes=40 * 2**20),
        cost_estimate=pl.CostEstimate(flops=17 * 6 * rank**3, bytes_accessed=6 * rank * rank, transcendentals=0),
    )(*parts)


def matrix_at(masks):
    core = lax.rem(lax.axis_index("fsdp"), 2)
    return lax.axis_index("ctx") ^ (masks[0] + (masks[1] - masks[0]) * core)


def last_kernel(update_scale, masks, waiting_masks, keeps, weights_ref, momentum_ref, peaks_ref, first_ref, second_ref, *refs):
    stores = []
    if keeps:
        fresh, factors = refs[-2:]
    else:
        out_ref, factors, fresh, left = refs[-4:]
    if waiting_masks is not None:
        stores.append(pltpu.make_async_copy(refs[0], out_ref.at[matrix_at(waiting_masks)], left.at[2]))
        stores[0].start()
    rank, cols = fresh.shape
    shard = lax.axis_index("fsdp")
    core = lax.rem(shard, 2)
    matrix = matrix_at(masks)
    for side, kept in enumerate(KEPT):
        for at, (row, column) in enumerate(kept):
            rows = slice(at * BLOCK, (at + 1) * BLOCK)
            block = jnp.where(core == side, first_ref[rows, :], second_ref[rows, :])
            factors[row * BLOCK : (row + 1) * BLOCK, column * BLOCK : (column + 1) * BLOCK] = block
            if row != column:
                factors[column * BLOCK : (column + 1) * BLOCK, row * BLOCK : (row + 1) * BLOCK] = block.T
    end = first_ref[HALF:, :].astype(jnp.float32)
    inverse = 1.0 / ((end[0:1, 0:1] + end[1:2, 0:1]) + end[2:3, 0:1])
    heads = cols // (KNOPE + VDIM)
    column = lax.broadcasted_iota(jnp.int32, (1, cols), 1)
    lane = lax.broadcasted_iota(jnp.int32, (1, BLOCK), 1)
    column_peaks = jnp.full((1, cols), clip_limit, jnp.float32)
    for head in range(heads):
        place = matrix * (BLOCK // BLOCKS) + shard * heads + head
        peak = jnp.max(jnp.where(lane == place, peaks_ref[0:1, :], 0.0), axis=1, keepdims=True)
        first = head * (KNOPE + VDIM)
        column_peaks = jnp.where((column >= first) & (column < first + KNOPE), peak, column_peaks)
    scale = jnp.sqrt(jnp.minimum(1.0, clip_limit / column_peaks))
    start = (momentum_ref[matrix].astype(jnp.float32) * inverse).astype(jnp.bfloat16)
    for at in range(rank // STRIP):
        rows = slice(at * STRIP, (at + 1) * STRIP)
        orthogonal = jnp.dot(factors[rows, :], start, preferred_element_type=jnp.float32)
        value = weights_ref[matrix, rows, :].astype(jnp.float32) - step_size * (update_scale * orthogonal)
        fresh[rows, :] = (value * scale).astype(jnp.bfloat16)
        if not keeps:
            stores.append(pltpu.make_async_copy(fresh.at[rows], out_ref.at[matrix, rows], left.at[at]))
            stores[-1].start()
    for store in stores:
        store.wait()


def last_product(update_scale, masks, weights, momentum, peaks, pair, before=None, waiting=None, keeps=False):
    rank, cols = weights.shape[1:]
    whole, outside = pl.BlockSpec(memory_space=pltpu.VMEM), pl.BlockSpec(memory_space=pl.ANY)
    waiting_masks, waiting_block = waiting or (None, None)
    extra = [] if waiting is None else [waiting_block]
    earlier = [] if before is None else [before]
    block = jax.ShapeDtypeStruct((rank, cols), weights.dtype)
    staging = [pltpu.VMEM((rank, cols), jnp.bfloat16), pltpu.SemaphoreType.DMA((3,))]
    return pl.pallas_call(
        functools.partial(last_kernel, update_scale, masks, waiting_masks, keeps),
        out_shape=block if keeps else jax.ShapeDtypeStruct(weights.shape, weights.dtype),
        in_specs=[whole] * (5 + len(extra)) + [outside] * len(earlier),
        out_specs=whole if keeps else outside,
        scratch_shapes=[pltpu.VMEM((rank, rank), jnp.bfloat16)] + ([] if keeps else staging),
        input_output_aliases={5 + len(extra): 0} if earlier else {},
        compiler_params=pltpu.CompilerParams(vmem_limit_bytes=24 * 2**20),
        cost_estimate=pl.CostEstimate(flops=2 * rank * rank * cols, bytes_accessed=6 * rank * cols, transcendentals=0),
    )(weights, momentum, peaks, *pair, *extra, *earlier)


def join_kernel(total_ref, arrived_ref, peaks_ref, peaks_arrived_ref, out_ref):
    out_ref[0:PART, :] = total_ref[...] + arrived_ref[...]
    out_ref[PART:, :] = jnp.maximum(peaks_ref[...], peaks_arrived_ref[...])


def join(*arrays):
    whole = pl.BlockSpec(memory_space=pltpu.VMEM)
    return pl.pallas_call(
        join_kernel,
        out_shape=jax.ShapeDtypeStruct((PART + TAIL, BLOCK), jnp.float32),
        in_specs=[whole] * 4,
        out_specs=whole,
        compiler_params=pltpu.CompilerParams(vmem_limit_bytes=8 * 2**20),
        cost_estimate=pl.CostEstimate(flops=PART * BLOCK, bytes_accessed=12 * PART * BLOCK, transcendentals=0),
    )(*arrays)


def crossed(value, axis, mask):
    return lax.ppermute(value, axis, [(at, at ^ mask) for at in range(lax.axis_size(axis))])


def along_z(value, mask):
    count = lax.axis_size("fsdp")
    zs = count // 2
    pairs = []
    for at in range(count):
        z_at, core = at // 2, at % 2
        partner = (((z_at - 2 * core) % zs ^ mask) + 2 * core) % zs
        pairs.append((at, 2 * partner + core))
    return lax.ppermute(value, "fsdp", pairs)


def by_core(value, axis, masks):
    count = lax.axis_size(axis)
    pairs = [
        (shard * count + at, shard * count + (at ^ masks[shard % 2]))
        for shard in range(lax.axis_size("fsdp"))
        for at in range(count)
    ]
    return lax.ppermute(value, ("fsdp", axis), pairs)


def swapped(value):
    return crossed(value, "fsdp", 1)


def on_device(weights, momentum, gradient, logit_max, layer_of):
    rank, cols = weights.shape[1:]
    fsdp = lax.axis_size("fsdp")
    layers = logit_max.shape[2]

    layer_match = jnp.arange(layers, dtype=jnp.int32)[None, :] == layer_of[:, None]
    peaks = jnp.max(jnp.where(layer_match[:, :, None], logit_max[0, 0][None], 0.0), axis=1)
    peaks = jnp.broadcast_to(peaks.reshape(1, BLOCK), (TAIL, BLOCK))

    keep, send = partial_gram(momentum, gradient)
    total = keep + swapped(send)
    total, peaks = lax.optimization_barrier((total, peaks))
    third, second, first = along_z(total, 3), along_z(total, 2), along_z(total, 1)
    total = (total + first) + (second + third)
    peaks = jnp.maximum(peaks, crossed(peaks, "ctx", 1))
    total, peaks = lax.optimization_barrier((total, peaks))
    mine = join(total, along_z(total, 7), peaks, crossed(peaks, "ctx", 3))
    halves = [mine] + [crossed(mine, "dp", mask) for mask in (1, 2, 3)]
    first, second, peaks = newton([piece for one in halves for piece in (one, swapped(one))], rank)
    update_scale = rms_factor * math.sqrt(max(rank, cols * fsdp))
    last = functools.partial(last_product, update_scale)
    peaks, late_momentum = lax.optimization_barrier((peaks, momentum))
    new_momentum = decayed(late_momentum, gradient)
    near = tuple(by_core(piece, "ctx", (1, 3)) for piece in (first, second))
    new_weights = last((0, 0), weights, new_momentum, peaks, (first, second))
    near_first, new_weights = lax.optimization_barrier((near[0], new_weights))
    far = by_core(near_first, "ctx", (3, 1))
    cross = swapped(near[1]), swapped(near_first)
    new_weights = last((1, 3), weights, new_momentum, peaks, (near_first, near[1]), new_weights)
    far, new_weights = lax.optimization_barrier((far, new_weights))
    far = far, swapped(far)
    waiting = last((3, 1), weights, new_momentum, peaks, cross, keeps=True)
    far, waiting = lax.optimization_barrier((far, waiting))
    new_weights = last((2, 2), weights, new_momentum, peaks, far, new_weights, ((3, 1), waiting))
    return (new_weights, new_momentum)


def solution(mesh):
    in_specs = (
        P(None, None, "fsdp"),
        P(None, None, "fsdp"),
        P(None, None, "fsdp"),
        P("dp", "ctx", None, None),
        P(),
    )
    out_specs = (P(None, None, "fsdp"), P(None, None, "fsdp"))
    return jax.shard_map(
        on_device, mesh=mesh, in_specs=in_specs, out_specs=out_specs, check_vma=False
    )
```

```python
import functools
import math

import jax
import jax.numpy as jnp
from jax import lax
from jax.experimental import pallas as pl
from jax.experimental.pallas import tpu as pltpu
from jax.sharding import PartitionSpec as P

KNOPE = 128
VDIM = 128
ITERS = 5

quintic_a = 3.4445
quintic_b = -4.775
quintic_c = 2.0315
momentum_decay = 0.95
step_size = 0.1
clip_limit = 100.0
norm_eps = 1e-07
rms_factor = 0.2

BLOCK = 128
BLOCKS = 4
HALF_BLOCK = 64
PART = 144
TAIL = 8
HALF = 640
END = 16
STRIP = 256
KEPT = [[(0, 0), (0, 1), (0, 2), (0, 3), (1, 1)], [(1, 2), (1, 3), (2, 2), (2, 3), (3, 3)]]


def decayed(momentum, gradient):
    return (momentum_decay * momentum.astype(jnp.float32) + gradient.astype(jnp.float32)).astype(jnp.bfloat16)


def aligned(index, to):
    return pl.multiple_of(index * to, to)


def partial_gram_kernel(momentum_ref, gradient_ref, keep_ref, send_ref, momentum, gradient, fresh, packed, arrived):
    matrix, dp_at, core = lax.axis_index("ctx"), lax.axis_index("dp"), lax.rem(lax.axis_index("fsdp"), 2)
    copies = []
    for at in (0, 2, 1):
        rows = pl.ds(aligned(lax.rem(dp_at + at, BLOCKS), BLOCK), BLOCK)
        pair = [
            pltpu.make_async_copy(source.at[matrix, rows], target.at[at], arrived.at[side, at])
            for side, (source, target) in enumerate(((momentum_ref, momentum), (gradient_ref, gradient)))
        ]
        for copy in pair:
            copy.start()
        copies.append((at, pair))
    for at, pair in copies:
        for copy in pair:
            copy.wait()
        fresh[at * BLOCK : (at + 1) * BLOCK, :] = decayed(momentum[at], gradient[at])

    def gram(left, right):
        return lax.dot_general(left, right, (((1,), (1,)), ((), ())), preferred_element_type=jnp.float32)

    early = dp_at < BLOCKS // 2
    far_rows = jnp.where(early, 0, 5)
    far_columns = jnp.where(early, 2, 0)
    packed[7 * HALF_BLOCK // 2 :, :] = gram(
        fresh[pl.ds(aligned(far_rows, BLOCK // 2), BLOCK // 2), :], fresh[pl.ds(aligned(far_columns, BLOCK), BLOCK), :]
    )
    own = gram(fresh[0:BLOCK, :], fresh[0:BLOCK, :])
    packed[0:HALF_BLOCK, :] = own[0:HALF_BLOCK, :]
    quarter = HALF_BLOCK // 2
    left_half = lax.broadcasted_iota(jnp.int32, (quarter, BLOCK), 1) < HALF_BLOCK
    third, fourth = own[2 * quarter : 3 * quarter, :], own[3 * quarter :, :]
    packed[HALF_BLOCK : 3 * quarter, :] = jnp.where(left_half, pltpu.roll(third, HALF_BLOCK, 1), fourth)
    packed[3 * quarter : 3 * quarter + BLOCK, :] = gram(fresh[0:BLOCK, :], fresh[BLOCK : 2 * BLOCK, :])
    keep_ref[...] = packed[pl.ds(aligned(core, PART), PART), :]
    send_ref[...] = packed[pl.ds(aligned(1 - core, PART), PART), :]


def partial_gram(momentum, gradient):
    rank, cols = momentum.shape[1:]
    shape = jax.ShapeDtypeStruct((PART, BLOCK), jnp.float32)
    blocks = pltpu.VMEM((3, BLOCK, cols), jnp.bfloat16)
    return pl.pallas_call(
        partial_gram_kernel,
        out_shape=(shape, shape),
        in_specs=[pl.BlockSpec(memory_space=pl.ANY)] * 2,
        out_specs=(pl.BlockSpec(memory_space=pltpu.VMEM),) * 2,
        scratch_shapes=[
            blocks,
            blocks,
            pltpu.VMEM((3 * BLOCK, cols), jnp.bfloat16),
            pltpu.VMEM((2 * PART, BLOCK), jnp.float32),
            pltpu.SemaphoreType.DMA((2, 3)),
        ],
        compiler_params=pltpu.CompilerParams(vmem_limit_bytes=53 * 2**20),
        cost_estimate=pl.CostEstimate(flops=4 * PART * BLOCK * cols, bytes_accessed=3 * rank * cols, transcendentals=0),
    )(momentum, gradient)


def split_in_two(value):
    high = value.astype(jnp.bfloat16)
    return high, (value - high.astype(jnp.float32)).astype(jnp.bfloat16)


def split_in_three(value):
    high = value.astype(jnp.bfloat16)
    rest = value - high.astype(jnp.float32)
    middle = rest.astype(jnp.bfloat16)
    return high, middle, (rest - middle.astype(jnp.float32)).astype(jnp.bfloat16)


def newton_kernel(*refs):
    parts, rest = [refs[2 * at : 2 * at + 2] for at in range(BLOCKS)], refs[2 * BLOCKS :]
    first_ref, second_ref, peaks_ref, packed, stacks, a_now, pair_a, pair_q, pair_b, pair_p, next_p = rest
    rank = a_now.shape[0]
    mid = rank // 2
    dp_at, core = lax.axis_index("dp"), lax.rem(lax.axis_index("fsdp"), 2)
    for turn, pair in enumerate(parts):
        for side, piece in enumerate(pair):
            half = core + side - 2 * core * side
            stacks[dp_at ^ turn, pl.ds(aligned(half, PART), PART), :] = piece[0:PART, :]
    peaks_ref[...] = functools.reduce(jnp.maximum, [pair[0][PART:, :] for pair in parts])

    quarter = HALF_BLOCK // 2
    rows_in = lax.broadcasted_iota(jnp.int32, (BLOCK, BLOCK), 0)
    columns_in = lax.broadcasted_iota(jnp.int32, (BLOCK, BLOCK), 1)
    missing = (rows_in >= HALF_BLOCK) & (columns_in < HALF_BLOCK)

    def own_block(block):
        low = stacks[block, HALF_BLOCK : 3 * quarter, :]
        return jnp.concatenate([stacks[block, 0:HALF_BLOCK, :], pltpu.roll(low, HALF_BLOCK, 1), low], axis=0)

    def beside(block):
        return stacks[block, 3 * quarter : 3 * quarter + BLOCK, :]

    def far(block):
        return stacks[block, 3 * quarter + BLOCK :, :]

    owns = [own_block(block) for block in range(BLOCKS)]
    diagonal = (owns[0] + owns[1]) + (owns[2] + owns[3])
    trace = jnp.sum(jnp.where(rows_in == columns_in, diagonal, 0.0))
    norm = jnp.sqrt(jnp.full((1, 1), trace, jnp.float32)) + norm_eps
    inverse = 1.0 / (norm * norm)

    def place(row, column, value):
        a_now[row * BLOCK : (row + 1) * BLOCK, column * BLOCK : (column + 1) * BLOCK] = value

    for block in range(BLOCKS):
        place(block, block, jnp.where(missing, owns[block].T, owns[block]))
        after = (block + 1) % BLOCKS
        place(block, after, beside(block))
        place(after, block, beside(block).T)
    for block in range(2):
        far_block = jnp.concatenate([far(block), far(block + 2)], axis=0)
        place(block, block + 2, far_block)
        place(block + 2, block, far_block.T)

    first, last = slice(0, mid), slice(mid, rank)
    rows_at = lax.broadcasted_iota(jnp.int32, (mid, rank), 0)
    columns_at = lax.broadcasted_iota(jnp.int32, (mid, rank), 1)
    shift = jnp.where(rows_at == columns_at, quintic_a, 0.0)
    dot = functools.partial(jnp.dot, preferred_element_type=jnp.float32)

    def keep(pair, rows, columns, value):
        strip = rows.start // mid
        pair[strip, 0, :, columns], pair[strip, 1, :, columns] = split_in_two(value)

    def product(left, right, rows, columns):
        strip = rows.start // mid
        high, low = [right[:, term, :, columns].reshape(rank, -1) for term in range(2)]
        both = dot(left[strip].reshape(rank, rank), high)
        return both[0:mid] + (both[mid:] + dot(left[strip, 0], low))

    def whole_product(left, right, target, finish=None):
        for rows, columns in ((first, slice(0, rank)), (last, last)):
            value = product(left, right, rows, columns)
            if finish is not None:
                value = finish(value, rows, columns)
            keep(target, rows, columns, value)
            if rows == first:
                keep(target, last, first, value[:, mid:].T)

    def to_factor(square, rows, columns):
        return shift[:, 0 : square.shape[1]] + quintic_b * a_now[rows, columns] + quintic_c * square

    def to_first_factor(square, rows, columns):
        return shift[:, 0 : square.shape[1]] + (quintic_b * inverse) * a_now[rows, columns] + (quintic_c * inverse) * (square * inverse)

    def scaled(value, rows, columns):
        return value * inverse

    def store(value, rows, columns):
        a_now[rows, columns] = value
        return value

    for rows in (first, last):
        keep(pair_a, rows, slice(0, rank), a_now[rows, :])
    for iteration in range(ITERS - 1):
        whole_product(pair_a, pair_a, pair_q, to_factor if iteration else to_first_factor)
        whole_product(pair_q, pair_a, pair_b, None if iteration else scaled)
        whole_product(pair_b, pair_q, pair_a, store)
        if iteration == 0:
            pair_p[...] = pair_q[...]
        else:
            whole_product(pair_p, pair_q, next_p)
            pair_p, next_p = next_p, pair_p
    whole_product(pair_a, pair_a, pair_q, to_factor)
    for rows, columns in ((first, slice(0, rank)), (last, last)):
        a_now[rows, columns] = product(pair_p, pair_q, rows, columns)
    for side, kept in enumerate(KEPT):
        for at, (row, column) in enumerate(kept):
            block = a_now[row * BLOCK : (row + 1) * BLOCK, column * BLOCK : (column + 1) * BLOCK]
            packed[side, at * BLOCK : (at + 1) * BLOCK, :] = block.astype(jnp.bfloat16)
    line = lax.broadcasted_iota(jnp.int32, (END, BLOCK), 0)
    spread = jnp.zeros((END, BLOCK), jnp.float32)
    for at, term in enumerate(split_in_three(norm)):
        spread = jnp.where(line == at, term.astype(jnp.float32), spread)
    for side in range(2):
        packed[side, HALF:, :] = spread.astype(jnp.bfloat16)
    first_ref[...] = packed[core]
    second_ref[...] = packed[1 - core]


def newton(parts, rank):
    whole = pl.BlockSpec(memory_space=pltpu.VMEM)
    pair = pltpu.VMEM((2, 2, rank // 2, rank), jnp.bfloat16)
    piece = jax.ShapeDtypeStruct((HALF + END, BLOCK), jnp.bfloat16)
    return pl.pallas_call(
        newton_kernel,
        out_shape=(piece, piece, jax.ShapeDtypeStruct((TAIL, BLOCK), jnp.float32)),
        in_specs=[whole] * len(parts),
        out_specs=(whole,) * 3,
        scratch_shapes=[
            pltpu.VMEM((2, HALF + END, BLOCK), jnp.bfloat16),
            pltpu.VMEM((BLOCKS, 2 * PART, BLOCK), jnp.float32),
            pltpu.VMEM((rank, rank), jnp.float32),
            pair,
            pair,
            pair,
            pair,
            pair,
        ],
        compiler_params=pltpu.CompilerParams(vmem_limit_bytes=40 * 2**20),
        cost_estimate=pl.CostEstimate(flops=17 * 6 * rank**3, bytes_accessed=6 * rank * rank, transcendentals=0),
    )(*parts)


def matrix_at(masks):
    core = lax.rem(lax.axis_index("fsdp"), 2)
    return lax.axis_index("ctx") ^ (masks[0] + (masks[1] - masks[0]) * core)


def last_kernel(update_scale, masks, waiting_masks, keeps, weights_ref, momentum_ref, peaks_ref, first_ref, second_ref, *refs):
    stores = []
    if keeps:
        fresh, factors = refs[-2:]
    else:
        out_ref, factors, fresh, left = refs[-4:]
    if waiting_masks is not None:
        stores.append(pltpu.make_async_copy(refs[0], out_ref.at[matrix_at(waiting_masks)], left.at[2]))
        stores[0].start()
    rank, cols = fresh.shape
    shard = lax.axis_index("fsdp")
    core = lax.rem(shard, 2)
    matrix = matrix_at(masks)
    for side, kept in enumerate(KEPT):
        for at, (row, column) in enumerate(kept):
            rows = slice(at * BLOCK, (at + 1) * BLOCK)
            block = jnp.where(core == side, first_ref[rows, :], second_ref[rows, :])
            factors[row * BLOCK : (row + 1) * BLOCK, column * BLOCK : (column + 1) * BLOCK] = block
            if row != column:
                factors[column * BLOCK : (column + 1) * BLOCK, row * BLOCK : (row + 1) * BLOCK] = block.T
    end = first_ref[HALF:, :].astype(jnp.float32)
    inverse = 1.0 / ((end[0:1, 0:1] + end[1:2, 0:1]) + end[2:3, 0:1])
    heads = cols // (KNOPE + VDIM)
    column = lax.broadcasted_iota(jnp.int32, (1, cols), 1)
    lane = lax.broadcasted_iota(jnp.int32, (1, BLOCK), 1)
    column_peaks = jnp.full((1, cols), clip_limit, jnp.float32)
    for head in range(heads):
        place = matrix * (BLOCK // BLOCKS) + shard * heads + head
        peak = jnp.max(jnp.where(lane == place, peaks_ref[0:1, :], 0.0), axis=1, keepdims=True)
        first = head * (KNOPE + VDIM)
        column_peaks = jnp.where((column >= first) & (column < first + KNOPE), peak, column_peaks)
    scale = jnp.sqrt(jnp.minimum(1.0, clip_limit / column_peaks))
    start = (momentum_ref[matrix].astype(jnp.float32) * inverse).astype(jnp.bfloat16)
    for at in range(rank // STRIP):
        rows = slice(at * STRIP, (at + 1) * STRIP)
        orthogonal = jnp.dot(factors[rows, :], start, preferred_element_type=jnp.float32)
        value = weights_ref[matrix, rows, :].astype(jnp.float32) - step_size * (update_scale * orthogonal)
        fresh[rows, :] = (value * scale).astype(jnp.bfloat16)
        if not keeps:
            stores.append(pltpu.make_async_copy(fresh.at[rows], out_ref.at[matrix, rows], left.at[at]))
            stores[-1].start()
    for store in stores:
        store.wait()


def last_product(update_scale, masks, weights, momentum, peaks, pair, before=None, waiting=None, keeps=False):
    rank, cols = weights.shape[1:]
    whole, outside = pl.BlockSpec(memory_space=pltpu.VMEM), pl.BlockSpec(memory_space=pl.ANY)
    waiting_masks, waiting_block = waiting or (None, None)
    extra = [] if waiting is None else [waiting_block]
    earlier = [] if before is None else [before]
    block = jax.ShapeDtypeStruct((rank, cols), weights.dtype)
    staging = [pltpu.VMEM((rank, cols), jnp.bfloat16), pltpu.SemaphoreType.DMA((3,))]
    return pl.pallas_call(
        functools.partial(last_kernel, update_scale, masks, waiting_masks, keeps),
        out_shape=block if keeps else jax.ShapeDtypeStruct(weights.shape, weights.dtype),
        in_specs=[whole] * (5 + len(extra)) + [outside] * len(earlier),
        out_specs=whole if keeps else outside,
        scratch_shapes=[pltpu.VMEM((rank, rank), jnp.bfloat16)] + ([] if keeps else staging),
        input_output_aliases={5 + len(extra): 0} if earlier else {},
        compiler_params=pltpu.CompilerParams(vmem_limit_bytes=24 * 2**20),
        cost_estimate=pl.CostEstimate(flops=2 * rank * rank * cols, bytes_accessed=6 * rank * cols, transcendentals=0),
    )(weights, momentum, peaks, *pair, *extra, *earlier)


def join_kernel(total_ref, arrived_ref, peaks_ref, peaks_arrived_ref, out_ref):
    out_ref[0:PART, :] = total_ref[...] + arrived_ref[...]
    out_ref[PART:, :] = jnp.maximum(peaks_ref[...], peaks_arrived_ref[...])


def join(*arrays):
    whole = pl.BlockSpec(memory_space=pltpu.VMEM)
    return pl.pallas_call(
        join_kernel,
        out_shape=jax.ShapeDtypeStruct((PART + TAIL, BLOCK), jnp.float32),
        in_specs=[whole] * 4,
        out_specs=whole,
        compiler_params=pltpu.CompilerParams(vmem_limit_bytes=8 * 2**20),
        cost_estimate=pl.CostEstimate(flops=PART * BLOCK, bytes_accessed=12 * PART * BLOCK, transcendentals=0),
    )(*arrays)


def crossed(value, axis, mask):
    return lax.ppermute(value, axis, [(at, at ^ mask) for at in range(lax.axis_size(axis))])


def along_z(value, mask):
    count = lax.axis_size("fsdp")
    zs = count // 2
    pairs = []
    for at in range(count):
        z_at, core = at // 2, at % 2
        partner = (((z_at - 2 * core) % zs ^ mask) + 2 * core) % zs
        pairs.append((at, 2 * partner + core))
    return lax.ppermute(value, "fsdp", pairs)


def by_core(value, axis, masks):
    count = lax.axis_size(axis)
    pairs = [
        (shard * count + at, shard * count + (at ^ masks[shard % 2]))
        for shard in range(lax.axis_size("fsdp"))
        for at in range(count)
    ]
    return lax.ppermute(value, ("fsdp", axis), pairs)


def swapped(value):
    return crossed(value, "fsdp", 1)


def on_device(weights, momentum, gradient, logit_max, layer_of):
    rank, cols = weights.shape[1:]
    fsdp = lax.axis_size("fsdp")
    layers = logit_max.shape[2]

    layer_match = jnp.arange(layers, dtype=jnp.int32)[None, :] == layer_of[:, None]
    peaks = jnp.max(jnp.where(layer_match[:, :, None], logit_max[0, 0][None], 0.0), axis=1)
    peaks = jnp.broadcast_to(peaks.reshape(1, BLOCK), (TAIL, BLOCK))

    keep, send = partial_gram(momentum, gradient)
    total = keep + swapped(send)
    total, peaks = lax.optimization_barrier((total, peaks))
    third, second, first = along_z(total, 3), along_z(total, 2), along_z(total, 1)
    total = (total + first) + (second + third)
    peaks = jnp.maximum(peaks, crossed(peaks, "ctx", 1))
    total, peaks = lax.optimization_barrier((total, peaks))
    mine = join(total, along_z(total, 7), peaks, crossed(peaks, "ctx", 3))
    halves = [mine] + [crossed(mine, "dp", mask) for mask in (1, 2, 3)]
    first, second, peaks = newton([piece for one in halves for piece in (one, swapped(one))], rank)
    update_scale = rms_factor * math.sqrt(max(rank, cols * fsdp))
    last = functools.partial(last_product, update_scale)
    peaks, late_momentum = lax.optimization_barrier((peaks, momentum))
    new_momentum = decayed(late_momentum, gradient)
    near_first = by_core(first, "ctx", (1, 3))
    late_second, new_momentum = lax.optimization_barrier((second, new_momentum))
    near = near_first, by_core(late_second, "ctx", (1, 3))
    new_weights = last((0, 0), weights, new_momentum, peaks, (first, second))
    near_first, new_weights = lax.optimization_barrier((near[0], new_weights))
    far = by_core(near_first, "ctx", (3, 1))
    cross = swapped(near[1]), swapped(near_first)
    new_weights = last((1, 3), weights, new_momentum, peaks, (near_first, near[1]), new_weights)
    far, new_weights = lax.optimization_barrier((far, new_weights))
    far = far, swapped(far)
    waiting = last((3, 1), weights, new_momentum, peaks, cross, keeps=True)
    far, waiting = lax.optimization_barrier((far, waiting))
    new_weights = last((2, 2), weights, new_momentum, peaks, far, new_weights, ((3, 1), waiting))
    return (new_weights, new_momentum)


def solution(mesh):
    in_specs = (
        P(None, None, "fsdp"),
        P(None, None, "fsdp"),
        P(None, None, "fsdp"),
        P("dp", "ctx", None, None),
        P(),
    )
    out_specs = (P(None, None, "fsdp"), P(None, None, "fsdp"))
    return jax.shard_map(
        on_device, mesh=mesh, in_specs=in_specs, out_specs=out_specs, check_vma=False
    )
```

```python
import functools
import math

import jax
import jax.numpy as jnp
from jax import lax
from jax.experimental import pallas as pl
from jax.experimental.pallas import tpu as pltpu
from jax.sharding import PartitionSpec as P

KNOPE = 128
VDIM = 128
ITERS = 5

quintic_a = 3.4445
quintic_b = -4.775
quintic_c = 2.0315
momentum_decay = 0.95
step_size = 0.1
clip_limit = 100.0
norm_eps = 1e-07
rms_factor = 0.2

BLOCK = 128
BLOCKS = 4
HALF_BLOCK = 64
PART = 144
TAIL = 8
HALF = 640
END = 16
STRIP = 256
KEPT = [[(0, 0), (0, 1), (0, 2), (0, 3), (1, 1)], [(1, 2), (1, 3), (2, 2), (2, 3), (3, 3)]]


def decayed(momentum, gradient):
    return (momentum_decay * momentum.astype(jnp.float32) + gradient.astype(jnp.float32)).astype(jnp.bfloat16)


def aligned(index, to):
    return pl.multiple_of(index * to, to)


def partial_gram_kernel(momentum_ref, gradient_ref, keep_ref, send_ref, momentum, gradient, fresh, packed, arrived):
    matrix, dp_at, core = lax.axis_index("ctx"), lax.axis_index("dp"), lax.rem(lax.axis_index("fsdp"), 2)
    copies = []
    for at in (0, 2, 1):
        rows = pl.ds(aligned(lax.rem(dp_at + at, BLOCKS), BLOCK), BLOCK)
        pair = [
            pltpu.make_async_copy(source.at[matrix, rows], target.at[at], arrived.at[side, at])
            for side, (source, target) in enumerate(((momentum_ref, momentum), (gradient_ref, gradient)))
        ]
        for copy in pair:
            copy.start()
        copies.append((at, pair))
    for at, pair in copies:
        for copy in pair:
            copy.wait()
        fresh[at * BLOCK : (at + 1) * BLOCK, :] = decayed(momentum[at], gradient[at])

    def gram(left, right):
        return lax.dot_general(left, right, (((1,), (1,)), ((), ())), preferred_element_type=jnp.float32)

    early = dp_at < BLOCKS // 2
    far_rows = jnp.where(early, 0, 5)
    far_columns = jnp.where(early, 2, 0)
    packed[7 * HALF_BLOCK // 2 :, :] = gram(
        fresh[pl.ds(aligned(far_rows, BLOCK // 2), BLOCK // 2), :], fresh[pl.ds(aligned(far_columns, BLOCK), BLOCK), :]
    )
    own = gram(fresh[0:BLOCK, :], fresh[0:BLOCK, :])
    packed[0:HALF_BLOCK, :] = own[0:HALF_BLOCK, :]
    quarter = HALF_BLOCK // 2
    left_half = lax.broadcasted_iota(jnp.int32, (quarter, BLOCK), 1) < HALF_BLOCK
    third, fourth = own[2 * quarter : 3 * quarter, :], own[3 * quarter :, :]
    packed[HALF_BLOCK : 3 * quarter, :] = jnp.where(left_half, pltpu.roll(third, HALF_BLOCK, 1), fourth)
    packed[3 * quarter : 3 * quarter + BLOCK, :] = gram(fresh[0:BLOCK, :], fresh[BLOCK : 2 * BLOCK, :])
    keep_ref[...] = packed[pl.ds(aligned(core, PART), PART), :]
    send_ref[...] = packed[pl.ds(aligned(1 - core, PART), PART), :]


def partial_gram(momentum, gradient):
    rank, cols = momentum.shape[1:]
    shape = jax.ShapeDtypeStruct((PART, BLOCK), jnp.float32)
    blocks = pltpu.VMEM((3, BLOCK, cols), jnp.bfloat16)
    return pl.pallas_call(
        partial_gram_kernel,
        out_shape=(shape, shape),
        in_specs=[pl.BlockSpec(memory_space=pl.ANY)] * 2,
        out_specs=(pl.BlockSpec(memory_space=pltpu.VMEM),) * 2,
        scratch_shapes=[
            blocks,
            blocks,
            pltpu.VMEM((3 * BLOCK, cols), jnp.bfloat16),
            pltpu.VMEM((2 * PART, BLOCK), jnp.float32),
            pltpu.SemaphoreType.DMA((2, 3)),
        ],
        compiler_params=pltpu.CompilerParams(vmem_limit_bytes=53 * 2**20),
        cost_estimate=pl.CostEstimate(flops=4 * PART * BLOCK * cols, bytes_accessed=3 * rank * cols, transcendentals=0),
    )(momentum, gradient)


def split_in_two(value):
    high = value.astype(jnp.bfloat16)
    return high, (value - high.astype(jnp.float32)).astype(jnp.bfloat16)


def split_in_three(value):
    high = value.astype(jnp.bfloat16)
    rest = value - high.astype(jnp.float32)
    middle = rest.astype(jnp.bfloat16)
    return high, middle, (rest - middle.astype(jnp.float32)).astype(jnp.bfloat16)


def newton_kernel(*refs):
    parts, rest = [refs[2 * at : 2 * at + 2] for at in range(BLOCKS)], refs[2 * BLOCKS :]
    first_ref, second_ref, peaks_ref, packed, stacks, a_now, pair_a, pair_q, pair_b, pair_p, next_p = rest
    rank = a_now.shape[0]
    mid = rank // 2
    dp_at, core = lax.axis_index("dp"), lax.rem(lax.axis_index("fsdp"), 2)
    for turn, pair in enumerate(parts):
        for side, piece in enumerate(pair):
            half = core + side - 2 * core * side
            stacks[dp_at ^ turn, pl.ds(aligned(half, PART), PART), :] = piece[0:PART, :]
    peaks_ref[...] = functools.reduce(jnp.maximum, [pair[0][PART:, :] for pair in parts])

    quarter = HALF_BLOCK // 2
    rows_in = lax.broadcasted_iota(jnp.int32, (BLOCK, BLOCK), 0)
    columns_in = lax.broadcasted_iota(jnp.int32, (BLOCK, BLOCK), 1)
    missing = (rows_in >= HALF_BLOCK) & (columns_in < HALF_BLOCK)

    def own_block(block):
        low = stacks[block, HALF_BLOCK : 3 * quarter, :]
        return jnp.concatenate([stacks[block, 0:HALF_BLOCK, :], pltpu.roll(low, HALF_BLOCK, 1), low], axis=0)

    def beside(block):
        return stacks[block, 3 * quarter : 3 * quarter + BLOCK, :]

    def far(block):
        return stacks[block, 3 * quarter + BLOCK :, :]

    owns = [own_block(block) for block in range(BLOCKS)]
    diagonal = (owns[0] + owns[1]) + (owns[2] + owns[3])
    trace = jnp.sum(jnp.where(rows_in == columns_in, diagonal, 0.0))
    norm = jnp.sqrt(jnp.full((1, 1), trace, jnp.float32)) + norm_eps
    inverse = 1.0 / (norm * norm)

    def place(row, column, value):
        a_now[row * BLOCK : (row + 1) * BLOCK, column * BLOCK : (column + 1) * BLOCK] = value

    for block in range(BLOCKS):
        place(block, block, jnp.where(missing, owns[block].T, owns[block]))
        after = (block + 1) % BLOCKS
        place(block, after, beside(block))
        place(after, block, beside(block).T)
    for block in range(2):
        far_block = jnp.concatenate([far(block), far(block + 2)], axis=0)
        place(block, block + 2, far_block)
        place(block + 2, block, far_block.T)

    first, last = slice(0, mid), slice(mid, rank)
    rows_at = lax.broadcasted_iota(jnp.int32, (mid, rank), 0)
    columns_at = lax.broadcasted_iota(jnp.int32, (mid, rank), 1)
    shift = jnp.where(rows_at == columns_at, quintic_a, 0.0)
    dot = functools.partial(jnp.dot, preferred_element_type=jnp.float32)

    def keep(pair, rows, columns, value):
        strip = rows.start // mid
        pair[strip, 0, :, columns], pair[strip, 1, :, columns] = split_in_two(value)

    def product(left, right, rows, columns):
        strip = rows.start // mid
        high, low = [right[:, term, :, columns].reshape(rank, -1) for term in range(2)]
        both = dot(left[strip].reshape(rank, rank), high)
        return both[0:mid] + (both[mid:] + dot(left[strip, 0], low))

    def whole_product(left, right, target, finish=None):
        for rows, columns in ((first, slice(0, rank)), (last, last)):
            value = product(left, right, rows, columns)
            if finish is not None:
                value = finish(value, rows, columns)
            keep(target, rows, columns, value)
            if rows == first:
                keep(target, last, first, value[:, mid:].T)

    def to_factor(square, rows, columns):
        return shift[:, 0 : square.shape[1]] + quintic_b * a_now[rows, columns] + quintic_c * square

    def to_first_factor(square, rows, columns):
        return shift[:, 0 : square.shape[1]] + (quintic_b * inverse) * a_now[rows, columns] + (quintic_c * inverse) * (square * inverse)

    def scaled(value, rows, columns):
        return value * inverse

    def store(value, rows, columns):
        a_now[rows, columns] = value
        return value

    for rows in (first, last):
        keep(pair_a, rows, slice(0, rank), a_now[rows, :])
    for iteration in range(ITERS - 1):
        whole_product(pair_a, pair_a, pair_q, to_factor if iteration else to_first_factor)
        whole_product(pair_q, pair_a, pair_b, None if iteration else scaled)
        whole_product(pair_b, pair_q, pair_a, store)
        if iteration == 0:
            pair_p[...] = pair_q[...]
        else:
            whole_product(pair_p, pair_q, next_p)
            pair_p, next_p = next_p, pair_p
    whole_product(pair_a, pair_a, pair_q, to_factor)
    for rows, columns in ((first, slice(0, rank)), (last, last)):
        a_now[rows, columns] = product(pair_p, pair_q, rows, columns)
    for side, kept in enumerate(KEPT):
        for at, (row, column) in enumerate(kept):
            block = a_now[row * BLOCK : (row + 1) * BLOCK, column * BLOCK : (column + 1) * BLOCK]
            packed[side, at * BLOCK : (at + 1) * BLOCK, :] = block.astype(jnp.bfloat16)
    line = lax.broadcasted_iota(jnp.int32, (END, BLOCK), 0)
    spread = jnp.zeros((END, BLOCK), jnp.float32)
    for at, term in enumerate(split_in_three(norm)):
        spread = jnp.where(line == at, term.astype(jnp.float32), spread)
    for side in range(2):
        packed[side, HALF:, :] = spread.astype(jnp.bfloat16)
    first_ref[...] = packed[core]
    second_ref[...] = packed[1 - core]


def newton(parts, rank):
    whole = pl.BlockSpec(memory_space=pltpu.VMEM)
    pair = pltpu.VMEM((2, 2, rank // 2, rank), jnp.bfloat16)
    piece = jax.ShapeDtypeStruct((HALF + END, BLOCK), jnp.bfloat16)
    return pl.pallas_call(
        newton_kernel,
        out_shape=(piece, piece, jax.ShapeDtypeStruct((TAIL, BLOCK), jnp.float32)),
        in_specs=[whole] * len(parts),
        out_specs=(whole,) * 3,
        scratch_shapes=[
            pltpu.VMEM((2, HALF + END, BLOCK), jnp.bfloat16),
            pltpu.VMEM((BLOCKS, 2 * PART, BLOCK), jnp.float32),
            pltpu.VMEM((rank, rank), jnp.float32),
            pair,
            pair,
            pair,
            pair,
            pair,
        ],
        compiler_params=pltpu.CompilerParams(vmem_limit_bytes=40 * 2**20),
        cost_estimate=pl.CostEstimate(flops=17 * 6 * rank**3, bytes_accessed=6 * rank * rank, transcendentals=0),
    )(*parts)


def matrix_at(masks):
    core = lax.rem(lax.axis_index("fsdp"), 2)
    return lax.axis_index("ctx") ^ (masks[0] + (masks[1] - masks[0]) * core)


def fill(factors, first_ref, second_ref):
    core = lax.rem(lax.axis_index("fsdp"), 2)
    for side, kept in enumerate(KEPT):
        for at, (row, column) in enumerate(kept):
            rows = slice(at * BLOCK, (at + 1) * BLOCK)
            block = jnp.where(core == side, first_ref[rows, :], second_ref[rows, :])
            factors[row * BLOCK : (row + 1) * BLOCK, column * BLOCK : (column + 1) * BLOCK] = block
            if row != column:
                factors[column * BLOCK : (column + 1) * BLOCK, row * BLOCK : (row + 1) * BLOCK] = block.T


def start_of(momentum, half_ref):
    end = half_ref[HALF:, :].astype(jnp.float32)
    inverse = 1.0 / ((end[0:1, 0:1] + end[1:2, 0:1]) + end[2:3, 0:1])
    return (momentum.astype(jnp.float32) * inverse).astype(jnp.bfloat16)


def scale_of(matrix, peaks_ref, cols):
    shard = lax.axis_index("fsdp")
    heads = cols // (KNOPE + VDIM)
    column = lax.broadcasted_iota(jnp.int32, (1, cols), 1)
    lane = lax.broadcasted_iota(jnp.int32, (1, BLOCK), 1)
    column_peaks = jnp.full((1, cols), clip_limit, jnp.float32)
    for head in range(heads):
        place = matrix * (BLOCK // BLOCKS) + shard * heads + head
        peak = jnp.max(jnp.where(lane == place, peaks_ref[0:1, :], 0.0), axis=1, keepdims=True)
        begin = head * (KNOPE + VDIM)
        column_peaks = jnp.where((column >= begin) & (column < begin + KNOPE), peak, column_peaks)
    return jnp.sqrt(jnp.minimum(1.0, clip_limit / column_peaks))


def fresh_rows(update_scale, weights, factors, start, scale):
    orthogonal = jnp.dot(factors, start, preferred_element_type=jnp.float32)
    value = weights.astype(jnp.float32) - step_size * (update_scale * orthogonal)
    return (value * scale).astype(jnp.bfloat16)


def last_kernel(update_scale, masks, weights_ref, momentum_ref, peaks_ref, first_ref, second_ref, *refs):
    out_ref, factors, fresh, left = refs[-4:]
    rank, cols = fresh.shape
    matrix = matrix_at(masks)
    fill(factors, first_ref, second_ref)
    start, scale = start_of(momentum_ref[matrix], first_ref), scale_of(matrix, peaks_ref, cols)
    stores = []
    for at in range(rank // STRIP):
        rows = slice(at * STRIP, (at + 1) * STRIP)
        fresh[rows, :] = fresh_rows(update_scale, weights_ref[matrix, rows, :], factors[rows, :], start, scale)
        stores.append(pltpu.make_async_copy(fresh.at[rows], out_ref.at[matrix, rows], left.at[at]))
        stores[-1].start()
    for store in stores:
        store.wait()


def waiting_kernel(update_scale, masks, next_masks, weights_ref, momentum_ref, peaks_ref, first_ref, second_ref, next_ref, out_ref, start_ref, scale_ref, factors):
    rank, cols = out_ref.shape
    matrix, following = matrix_at(masks), matrix_at(next_masks)
    fill(factors, first_ref, second_ref)
    start, scale = start_of(momentum_ref[matrix], first_ref), scale_of(matrix, peaks_ref, cols)
    for at in range(rank // STRIP):
        rows = slice(at * STRIP, (at + 1) * STRIP)
        out_ref[rows, :] = fresh_rows(update_scale, weights_ref[matrix, rows, :], factors[rows, :], start, scale)
    start_ref[...] = start_of(momentum_ref[following], next_ref)
    scale_ref[...] = jnp.broadcast_to(scale_of(following, peaks_ref, cols), scale_ref.shape)


def closing_kernel(update_scale, masks, waiting_masks, weights_ref, first_ref, second_ref, waiting_ref, start_ref, scale_ref, before_ref, out_ref, factors, fresh, left):
    rank = fresh.shape[0]
    matrix = matrix_at(masks)
    stores = [pltpu.make_async_copy(waiting_ref, out_ref.at[matrix_at(waiting_masks)], left.at[2])]
    stores[0].start()
    fill(factors, first_ref, second_ref)
    for at in range(rank // STRIP):
        rows = slice(at * STRIP, (at + 1) * STRIP)
        fresh[rows, :] = fresh_rows(update_scale, weights_ref[matrix, rows, :], factors[rows, :], start_ref[...], scale_ref[0:1, :])
        stores.append(pltpu.make_async_copy(fresh.at[rows], out_ref.at[matrix, rows], left.at[at]))
        stores[-1].start()
    for store in stores:
        store.wait()


def last_call(kernel, weights, inside, before, outs=None):
    rank, cols = weights.shape[1:]
    whole, outside = pl.BlockSpec(memory_space=pltpu.VMEM), pl.BlockSpec(memory_space=pl.ANY)
    earlier = [] if before is None else [before]
    staging = [pltpu.VMEM((rank, cols), jnp.bfloat16), pltpu.SemaphoreType.DMA((3,))]
    return pl.pallas_call(
        kernel,
        out_shape=outs or jax.ShapeDtypeStruct(weights.shape, weights.dtype),
        in_specs=[whole] * (1 + len(inside)) + [outside] * len(earlier),
        out_specs=(whole,) * len(outs) if outs else outside,
        scratch_shapes=[pltpu.VMEM((rank, rank), jnp.bfloat16)] + ([] if outs else staging),
        input_output_aliases={1 + len(inside): 0} if earlier else {},
        compiler_params=pltpu.CompilerParams(vmem_limit_bytes=24 * 2**20),
        cost_estimate=pl.CostEstimate(flops=2 * rank * rank * cols, bytes_accessed=6 * rank * cols, transcendentals=0),
    )(weights, *inside, *earlier)


def join_kernel(total_ref, arrived_ref, peaks_ref, peaks_arrived_ref, out_ref):
    out_ref[0:PART, :] = total_ref[...] + arrived_ref[...]
    out_ref[PART:, :] = jnp.maximum(peaks_ref[...], peaks_arrived_ref[...])


def join(*arrays):
    whole = pl.BlockSpec(memory_space=pltpu.VMEM)
    return pl.pallas_call(
        join_kernel,
        out_shape=jax.ShapeDtypeStruct((PART + TAIL, BLOCK), jnp.float32),
        in_specs=[whole] * 4,
        out_specs=whole,
        compiler_params=pltpu.CompilerParams(vmem_limit_bytes=8 * 2**20),
        cost_estimate=pl.CostEstimate(flops=PART * BLOCK, bytes_accessed=12 * PART * BLOCK, transcendentals=0),
    )(*arrays)


def crossed(value, axis, mask):
    return lax.ppermute(value, axis, [(at, at ^ mask) for at in range(lax.axis_size(axis))])


def along_z(value, mask):
    count = lax.axis_size("fsdp")
    zs = count // 2
    pairs = []
    for at in range(count):
        z_at, core = at // 2, at % 2
        partner = (((z_at - 2 * core) % zs ^ mask) + 2 * core) % zs
        pairs.append((at, 2 * partner + core))
    return lax.ppermute(value, "fsdp", pairs)


def by_core(value, axis, masks):
    count = lax.axis_size(axis)
    pairs = [
        (shard * count + at, shard * count + (at ^ masks[shard % 2]))
        for shard in range(lax.axis_size("fsdp"))
        for at in range(count)
    ]
    return lax.ppermute(value, ("fsdp", axis), pairs)


def swapped(value):
    return crossed(value, "fsdp", 1)


def on_device(weights, momentum, gradient, logit_max, layer_of):
    rank, cols = weights.shape[1:]
    fsdp = lax.axis_size("fsdp")
    layers = logit_max.shape[2]

    layer_match = jnp.arange(layers, dtype=jnp.int32)[None, :] == layer_of[:, None]
    peaks = jnp.max(jnp.where(layer_match[:, :, None], logit_max[0, 0][None], 0.0), axis=1)
    peaks = jnp.broadcast_to(peaks.reshape(1, BLOCK), (TAIL, BLOCK))

    keep, send = partial_gram(momentum, gradient)
    total = keep + swapped(send)
    total, peaks = lax.optimization_barrier((total, peaks))
    third, second, first = along_z(total, 3), along_z(total, 2), along_z(total, 1)
    total = (total + first) + (second + third)
    peaks = jnp.maximum(peaks, crossed(peaks, "ctx", 1))
    total, peaks = lax.optimization_barrier((total, peaks))
    mine = join(total, along_z(total, 7), peaks, crossed(peaks, "ctx", 3))
    halves = [mine] + [crossed(mine, "dp", mask) for mask in (1, 2, 3)]
    first, second, peaks = newton([piece for one in halves for piece in (one, swapped(one))], rank)
    update_scale = rms_factor * math.sqrt(max(rank, cols * fsdp))
    peaks, late_momentum = lax.optimization_barrier((peaks, momentum))
    new_momentum = decayed(late_momentum, gradient)

    def last(masks, pair, before=None):
        kernel = functools.partial(last_kernel, update_scale, masks)
        return last_call(kernel, weights, [new_momentum, peaks, *pair], before)

    near = tuple(by_core(piece, "ctx", (1, 3)) for piece in (first, second))
    new_weights = last((0, 0), (first, second))
    near_first, new_weights = lax.optimization_barrier((near[0], new_weights))
    far = by_core(near_first, "ctx", (3, 1))
    cross = swapped(near[1]), swapped(near_first)
    new_weights = last((1, 3), (near_first, near[1]), new_weights)
    far, new_weights = lax.optimization_barrier((far, new_weights))
    far_too = swapped(far)
    block = jax.ShapeDtypeStruct((rank, cols), jnp.bfloat16)
    waiting = last_call(
        functools.partial(waiting_kernel, update_scale, (3, 1), (2, 2)),
        weights,
        [new_momentum, peaks, *cross, far],
        None,
        (block, block, jax.ShapeDtypeStruct((8, cols), jnp.float32)),
    )
    far_too, waiting = lax.optimization_barrier((far_too, waiting))
    closing = functools.partial(closing_kernel, update_scale, (2, 2), (3, 1))
    new_weights = last_call(closing, weights, [far, far_too, *waiting], new_weights)
    return (new_weights, new_momentum)


def solution(mesh):
    in_specs = (
        P(None, None, "fsdp"),
        P(None, None, "fsdp"),
        P(None, None, "fsdp"),
        P("dp", "ctx", None, None),
        P(),
    )
    out_specs = (P(None, None, "fsdp"), P(None, None, "fsdp"))
    return jax.shard_map(
        on_device, mesh=mesh, in_specs=in_specs, out_specs=out_specs, check_vma=False
    )
```

```python
import functools
import math

import jax
import jax.numpy as jnp
from jax import lax
from jax.experimental import pallas as pl
from jax.experimental.pallas import tpu as pltpu
from jax.sharding import PartitionSpec as P

KNOPE = 128
VDIM = 128
ITERS = 5

quintic_a = 3.4445
quintic_b = -4.775
quintic_c = 2.0315
momentum_decay = 0.95
step_size = 0.1
clip_limit = 100.0
norm_eps = 1e-07
rms_factor = 0.2

BLOCK = 128
BLOCKS = 4
HALF_BLOCK = 64
PART = 144
TAIL = 8
HALF = 640
END = 16
STRIP = 256
TURNS = (0, 1, 3, 2)
KEPT = [[(0, 0), (0, 1), (0, 2), (0, 3), (1, 1)], [(1, 2), (1, 3), (2, 2), (2, 3), (3, 3)]]


def decayed(momentum, gradient):
    return (momentum_decay * momentum.astype(jnp.float32) + gradient.astype(jnp.float32)).astype(jnp.bfloat16)


def aligned(index, to):
    return pl.multiple_of(index * to, to)


def partial_gram_kernel(momentum_ref, gradient_ref, keep_ref, send_ref, momentum, gradient, fresh, packed, arrived):
    matrix, dp_at, core = lax.axis_index("ctx"), lax.axis_index("dp"), lax.rem(lax.axis_index("fsdp"), 2)
    copies = []
    for at in (0, 2, 1):
        rows = pl.ds(aligned(lax.rem(dp_at + at, BLOCKS), BLOCK), BLOCK)
        pair = [
            pltpu.make_async_copy(source.at[matrix, rows], target.at[at], arrived.at[side, at])
            for side, (source, target) in enumerate(((momentum_ref, momentum), (gradient_ref, gradient)))
        ]
        for copy in pair:
            copy.start()
        copies.append((at, pair))
    for at, pair in copies:
        for copy in pair:
            copy.wait()
        fresh[at * BLOCK : (at + 1) * BLOCK, :] = decayed(momentum[at], gradient[at])

    def gram(left, right):
        return lax.dot_general(left, right, (((1,), (1,)), ((), ())), preferred_element_type=jnp.float32)

    early = dp_at < BLOCKS // 2
    far_rows = jnp.where(early, 0, 5)
    far_columns = jnp.where(early, 2, 0)
    packed[7 * HALF_BLOCK // 2 :, :] = gram(
        fresh[pl.ds(aligned(far_rows, BLOCK // 2), BLOCK // 2), :], fresh[pl.ds(aligned(far_columns, BLOCK), BLOCK), :]
    )
    own = gram(fresh[0:BLOCK, :], fresh[0:BLOCK, :])
    packed[0:HALF_BLOCK, :] = own[0:HALF_BLOCK, :]
    quarter = HALF_BLOCK // 2
    left_half = lax.broadcasted_iota(jnp.int32, (quarter, BLOCK), 1) < HALF_BLOCK
    third, fourth = own[2 * quarter : 3 * quarter, :], own[3 * quarter :, :]
    packed[HALF_BLOCK : 3 * quarter, :] = jnp.where(left_half, pltpu.roll(third, HALF_BLOCK, 1), fourth)
    packed[3 * quarter : 3 * quarter + BLOCK, :] = gram(fresh[0:BLOCK, :], fresh[BLOCK : 2 * BLOCK, :])
    keep_ref[...] = packed[pl.ds(aligned(core, PART), PART), :]
    send_ref[...] = packed[pl.ds(aligned(1 - core, PART), PART), :]


def partial_gram(momentum, gradient):
    rank, cols = momentum.shape[1:]
    shape = jax.ShapeDtypeStruct((PART, BLOCK), jnp.float32)
    blocks = pltpu.VMEM((3, BLOCK, cols), jnp.bfloat16)
    return pl.pallas_call(
        partial_gram_kernel,
        out_shape=(shape, shape),
        in_specs=[pl.BlockSpec(memory_space=pl.ANY)] * 2,
        out_specs=(pl.BlockSpec(memory_space=pltpu.VMEM),) * 2,
        scratch_shapes=[
            blocks,
            blocks,
            pltpu.VMEM((3 * BLOCK, cols), jnp.bfloat16),
            pltpu.VMEM((2 * PART, BLOCK), jnp.float32),
            pltpu.SemaphoreType.DMA((2, 3)),
        ],
        compiler_params=pltpu.CompilerParams(vmem_limit_bytes=53 * 2**20),
        cost_estimate=pl.CostEstimate(flops=4 * PART * BLOCK * cols, bytes_accessed=3 * rank * cols, transcendentals=0),
    )(momentum, gradient)


def split_in_two(value):
    high = value.astype(jnp.bfloat16)
    return high, (value - high.astype(jnp.float32)).astype(jnp.bfloat16)


def split_in_three(value):
    high = value.astype(jnp.bfloat16)
    rest = value - high.astype(jnp.float32)
    middle = rest.astype(jnp.bfloat16)
    return high, middle, (rest - middle.astype(jnp.float32)).astype(jnp.bfloat16)


def newton_kernel(*refs):
    parts, rest = [refs[2 * at : 2 * at + 2] for at in range(BLOCKS)], refs[2 * BLOCKS :]
    first_ref, second_ref, peaks_ref, packed, stacks, a_now, pair_a, pair_q, pair_b, pair_p, next_p = rest
    rank = a_now.shape[0]
    mid = rank // 2
    dp_at, core = lax.axis_index("dp"), lax.rem(lax.axis_index("fsdp"), 2)
    for turn, pair in zip(TURNS, parts):
        for side, piece in enumerate(pair):
            half = core + side - 2 * core * side
            stacks[dp_at ^ turn, pl.ds(aligned(half, PART), PART), :] = piece[0:PART, :]
    peaks_ref[...] = functools.reduce(jnp.maximum, [pair[0][PART:, :] for pair in parts])

    quarter = HALF_BLOCK // 2
    rows_in = lax.broadcasted_iota(jnp.int32, (BLOCK, BLOCK), 0)
    columns_in = lax.broadcasted_iota(jnp.int32, (BLOCK, BLOCK), 1)
    missing = (rows_in >= HALF_BLOCK) & (columns_in < HALF_BLOCK)

    def own_block(block):
        low = stacks[block, HALF_BLOCK : 3 * quarter, :]
        return jnp.concatenate([stacks[block, 0:HALF_BLOCK, :], pltpu.roll(low, HALF_BLOCK, 1), low], axis=0)

    def beside(block):
        return stacks[block, 3 * quarter : 3 * quarter + BLOCK, :]

    def far(block):
        return stacks[block, 3 * quarter + BLOCK :, :]

    owns = [own_block(block) for block in range(BLOCKS)]
    diagonal = (owns[0] + owns[1]) + (owns[2] + owns[3])
    trace = jnp.sum(jnp.where(rows_in == columns_in, diagonal, 0.0))
    norm = jnp.sqrt(jnp.full((1, 1), trace, jnp.float32)) + norm_eps
    inverse = 1.0 / (norm * norm)

    def place(row, column, value):
        a_now[row * BLOCK : (row + 1) * BLOCK, column * BLOCK : (column + 1) * BLOCK] = value

    for block in range(BLOCKS):
        place(block, block, jnp.where(missing, owns[block].T, owns[block]))
        after = (block + 1) % BLOCKS
        place(block, after, beside(block))
        place(after, block, beside(block).T)
    for block in range(2):
        far_block = jnp.concatenate([far(block), far(block + 2)], axis=0)
        place(block, block + 2, far_block)
        place(block + 2, block, far_block.T)

    first, last = slice(0, mid), slice(mid, rank)
    rows_at = lax.broadcasted_iota(jnp.int32, (mid, rank), 0)
    columns_at = lax.broadcasted_iota(jnp.int32, (mid, rank), 1)
    shift = jnp.where(rows_at == columns_at, quintic_a, 0.0)
    dot = functools.partial(jnp.dot, preferred_element_type=jnp.float32)

    def keep(pair, rows, columns, value):
        strip = rows.start // mid
        pair[strip, 0, :, columns], pair[strip, 1, :, columns] = split_in_two(value)

    def product(left, right, rows, columns):
        strip = rows.start // mid
        high, low = [right[:, term, :, columns].reshape(rank, -1) for term in range(2)]
        both = dot(left[strip].reshape(rank, rank), high)
        return both[0:mid] + (both[mid:] + dot(left[strip, 0], low))

    def whole_product(left, right, target, finish=None):
        for rows, columns in ((first, slice(0, rank)), (last, last)):
            value = product(left, right, rows, columns)
            if finish is not None:
                value = finish(value, rows, columns)
            keep(target, rows, columns, value)
            if rows == first:
                keep(target, last, first, value[:, mid:].T)

    def to_factor(square, rows, columns):
        return shift[:, 0 : square.shape[1]] + quintic_b * a_now[rows, columns] + quintic_c * square

    def to_first_factor(square, rows, columns):
        return shift[:, 0 : square.shape[1]] + (quintic_b * inverse) * a_now[rows, columns] + (quintic_c * inverse) * (square * inverse)

    def scaled(value, rows, columns):
        return value * inverse

    def store(value, rows, columns):
        a_now[rows, columns] = value
        return value

    for rows in (first, last):
        keep(pair_a, rows, slice(0, rank), a_now[rows, :])
    for iteration in range(ITERS - 1):
        whole_product(pair_a, pair_a, pair_q, to_factor if iteration else to_first_factor)
        whole_product(pair_q, pair_a, pair_b, None if iteration else scaled)
        whole_product(pair_b, pair_q, pair_a, store)
        if iteration == 0:
            pair_p[...] = pair_q[...]
        else:
            whole_product(pair_p, pair_q, next_p)
            pair_p, next_p = next_p, pair_p
    whole_product(pair_a, pair_a, pair_q, to_factor)
    for rows, columns in ((first, slice(0, rank)), (last, last)):
        a_now[rows, columns] = product(pair_p, pair_q, rows, columns)
    for side, kept in enumerate(KEPT):
        for at, (row, column) in enumerate(kept):
            block = a_now[row * BLOCK : (row + 1) * BLOCK, column * BLOCK : (column + 1) * BLOCK]
            packed[side, at * BLOCK : (at + 1) * BLOCK, :] = block.astype(jnp.bfloat16)
    line = lax.broadcasted_iota(jnp.int32, (END, BLOCK), 0)
    spread = jnp.zeros((END, BLOCK), jnp.float32)
    for at, term in enumerate(split_in_three(norm)):
        spread = jnp.where(line == at, term.astype(jnp.float32), spread)
    for side in range(2):
        packed[side, HALF:, :] = spread.astype(jnp.bfloat16)
    first_ref[...] = packed[core]
    second_ref[...] = packed[1 - core]


def newton(parts, rank):
    whole = pl.BlockSpec(memory_space=pltpu.VMEM)
    pair = pltpu.VMEM((2, 2, rank // 2, rank), jnp.bfloat16)
    piece = jax.ShapeDtypeStruct((HALF + END, BLOCK), jnp.bfloat16)
    return pl.pallas_call(
        newton_kernel,
        out_shape=(piece, piece, jax.ShapeDtypeStruct((TAIL, BLOCK), jnp.float32)),
        in_specs=[whole] * len(parts),
        out_specs=(whole,) * 3,
        scratch_shapes=[
            pltpu.VMEM((2, HALF + END, BLOCK), jnp.bfloat16),
            pltpu.VMEM((BLOCKS, 2 * PART, BLOCK), jnp.float32),
            pltpu.VMEM((rank, rank), jnp.float32),
            pair,
            pair,
            pair,
            pair,
            pair,
        ],
        compiler_params=pltpu.CompilerParams(vmem_limit_bytes=40 * 2**20),
        cost_estimate=pl.CostEstimate(flops=17 * 6 * rank**3, bytes_accessed=6 * rank * rank, transcendentals=0),
    )(*parts)


def matrix_at(masks):
    core = lax.rem(lax.axis_index("fsdp"), 2)
    return lax.axis_index("ctx") ^ (masks[0] + (masks[1] - masks[0]) * core)


def fill(factors, first_ref, second_ref):
    core = lax.rem(lax.axis_index("fsdp"), 2)
    for side, kept in enumerate(KEPT):
        for at, (row, column) in enumerate(kept):
            rows = slice(at * BLOCK, (at + 1) * BLOCK)
            block = jnp.where(core == side, first_ref[rows, :], second_ref[rows, :])
            factors[row * BLOCK : (row + 1) * BLOCK, column * BLOCK : (column + 1) * BLOCK] = block
            if row != column:
                factors[column * BLOCK : (column + 1) * BLOCK, row * BLOCK : (row + 1) * BLOCK] = block.T


def start_of(momentum, half_ref):
    end = half_ref[HALF:, :].astype(jnp.float32)
    inverse = 1.0 / ((end[0:1, 0:1] + end[1:2, 0:1]) + end[2:3, 0:1])
    return (momentum.astype(jnp.float32) * inverse).astype(jnp.bfloat16)


def scale_of(matrix, peaks_ref, cols):
    shard = lax.axis_index("fsdp")
    heads = cols // (KNOPE + VDIM)
    column = lax.broadcasted_iota(jnp.int32, (1, cols), 1)
    lane = lax.broadcasted_iota(jnp.int32, (1, BLOCK), 1)
    column_peaks = jnp.full((1, cols), clip_limit, jnp.float32)
    for head in range(heads):
        place = matrix * (BLOCK // BLOCKS) + shard * heads + head
        peak = jnp.max(jnp.where(lane == place, peaks_ref[0:1, :], 0.0), axis=1, keepdims=True)
        begin = head * (KNOPE + VDIM)
        column_peaks = jnp.where((column >= begin) & (column < begin + KNOPE), peak, column_peaks)
    return jnp.sqrt(jnp.minimum(1.0, clip_limit / column_peaks))


def fresh_rows(update_scale, weights, factors, start, scale):
    orthogonal = jnp.dot(factors, start, preferred_element_type=jnp.float32)
    value = weights.astype(jnp.float32) - step_size * (update_scale * orthogonal)
    return (value * scale).astype(jnp.bfloat16)


def last_kernel(update_scale, masks, weights_ref, momentum_ref, peaks_ref, first_ref, second_ref, *refs):
    out_ref, factors, fresh, left = refs[-4:]
    rank, cols = fresh.shape
    matrix = matrix_at(masks)
    fill(factors, first_ref, second_ref)
    start, scale = start_of(momentum_ref[matrix], first_ref), scale_of(matrix, peaks_ref, cols)
    stores = []
    for at in range(rank // STRIP):
        rows = slice(at * STRIP, (at + 1) * STRIP)
        fresh[rows, :] = fresh_rows(update_scale, weights_ref[matrix, rows, :], factors[rows, :], start, scale)
        stores.append(pltpu.make_async_copy(fresh.at[rows], out_ref.at[matrix, rows], left.at[at]))
        stores[-1].start()
    for store in stores:
        store.wait()


def waiting_kernel(update_scale, masks, next_masks, weights_ref, momentum_ref, peaks_ref, first_ref, second_ref, next_ref, out_ref, start_ref, scale_ref, factors):
    rank, cols = out_ref.shape
    matrix, following = matrix_at(masks), matrix_at(next_masks)
    fill(factors, first_ref, second_ref)
    start, scale = start_of(momentum_ref[matrix], first_ref), scale_of(matrix, peaks_ref, cols)
    for at in range(rank // STRIP):
        rows = slice(at * STRIP, (at + 1) * STRIP)
        out_ref[rows, :] = fresh_rows(update_scale, weights_ref[matrix, rows, :], factors[rows, :], start, scale)
    start_ref[...] = start_of(momentum_ref[following], next_ref)
    scale_ref[...] = jnp.broadcast_to(scale_of(following, peaks_ref, cols), scale_ref.shape)


def closing_kernel(update_scale, masks, waiting_masks, weights_ref, first_ref, second_ref, waiting_ref, start_ref, scale_ref, before_ref, out_ref, factors, fresh, left):
    rank = fresh.shape[0]
    matrix = matrix_at(masks)
    stores = [pltpu.make_async_copy(waiting_ref, out_ref.at[matrix_at(waiting_masks)], left.at[2])]
    stores[0].start()
    fill(factors, first_ref, second_ref)
    for at in range(rank // STRIP):
        rows = slice(at * STRIP, (at + 1) * STRIP)
        fresh[rows, :] = fresh_rows(update_scale, weights_ref[matrix, rows, :], factors[rows, :], start_ref[...], scale_ref[0:1, :])
        stores.append(pltpu.make_async_copy(fresh.at[rows], out_ref.at[matrix, rows], left.at[at]))
        stores[-1].start()
    for store in stores:
        store.wait()


def last_call(kernel, weights, inside, before, outs=None):
    rank, cols = weights.shape[1:]
    whole, outside = pl.BlockSpec(memory_space=pltpu.VMEM), pl.BlockSpec(memory_space=pl.ANY)
    earlier = [] if before is None else [before]
    staging = [pltpu.VMEM((rank, cols), jnp.bfloat16), pltpu.SemaphoreType.DMA((3,))]
    return pl.pallas_call(
        kernel,
        out_shape=outs or jax.ShapeDtypeStruct(weights.shape, weights.dtype),
        in_specs=[whole] * (1 + len(inside)) + [outside] * len(earlier),
        out_specs=(whole,) * len(outs) if outs else outside,
        scratch_shapes=[pltpu.VMEM((rank, rank), jnp.bfloat16)] + ([] if outs else staging),
        input_output_aliases={1 + len(inside): 0} if earlier else {},
        compiler_params=pltpu.CompilerParams(vmem_limit_bytes=24 * 2**20),
        cost_estimate=pl.CostEstimate(flops=2 * rank * rank * cols, bytes_accessed=6 * rank * cols, transcendentals=0),
    )(weights, *inside, *earlier)


def join_kernel(total_ref, arrived_ref, peaks_ref, peaks_arrived_ref, out_ref):
    out_ref[0:PART, :] = total_ref[...] + arrived_ref[...]
    out_ref[PART:, :] = jnp.maximum(peaks_ref[...], peaks_arrived_ref[...])


def join(*arrays):
    whole = pl.BlockSpec(memory_space=pltpu.VMEM)
    return pl.pallas_call(
        join_kernel,
        out_shape=jax.ShapeDtypeStruct((PART + TAIL, BLOCK), jnp.float32),
        in_specs=[whole] * 4,
        out_specs=whole,
        compiler_params=pltpu.CompilerParams(vmem_limit_bytes=8 * 2**20),
        cost_estimate=pl.CostEstimate(flops=PART * BLOCK, bytes_accessed=12 * PART * BLOCK, transcendentals=0),
    )(*arrays)


def crossed(value, axis, mask):
    return lax.ppermute(value, axis, [(at, at ^ mask) for at in range(lax.axis_size(axis))])


def along_z(value, mask):
    count = lax.axis_size("fsdp")
    zs = count // 2
    pairs = []
    for at in range(count):
        z_at, core = at // 2, at % 2
        partner = (((z_at - 2 * core) % zs ^ mask) + 2 * core) % zs
        pairs.append((at, 2 * partner + core))
    return lax.ppermute(value, "fsdp", pairs)


def by_core(value, axis, masks):
    count = lax.axis_size(axis)
    pairs = [
        (shard * count + at, shard * count + (at ^ masks[shard % 2]))
        for shard in range(lax.axis_size("fsdp"))
        for at in range(count)
    ]
    return lax.ppermute(value, ("fsdp", axis), pairs)


def swapped(value):
    return crossed(value, "fsdp", 1)


def on_device(weights, momentum, gradient, logit_max, layer_of):
    rank, cols = weights.shape[1:]
    fsdp = lax.axis_size("fsdp")
    layers = logit_max.shape[2]

    layer_match = jnp.arange(layers, dtype=jnp.int32)[None, :] == layer_of[:, None]
    peaks = jnp.max(jnp.where(layer_match[:, :, None], logit_max[0, 0][None], 0.0), axis=1)
    peaks = jnp.broadcast_to(peaks.reshape(1, BLOCK), (TAIL, BLOCK))

    keep, send = partial_gram(momentum, gradient)
    total = keep + swapped(send)
    total, peaks = lax.optimization_barrier((total, peaks))
    third, second, first = along_z(total, 3), along_z(total, 2), along_z(total, 1)
    total = (total + first) + (second + third)
    peaks = jnp.maximum(peaks, crossed(peaks, "ctx", 1))
    total, peaks = lax.optimization_barrier((total, peaks))
    mine = join(total, along_z(total, 7), peaks, crossed(peaks, "ctx", 3))
    halves = [mine] + [crossed(mine, "dp", mask) for mask in TURNS[1:]]
    first, second, peaks = newton([piece for one in halves for piece in (one, swapped(one))], rank)
    update_scale = rms_factor * math.sqrt(max(rank, cols * fsdp))
    peaks, late_momentum = lax.optimization_barrier((peaks, momentum))
    new_momentum = decayed(late_momentum, gradient)

    def last(masks, pair, before=None):
        kernel = functools.partial(last_kernel, update_scale, masks)
        return last_call(kernel, weights, [new_momentum, peaks, *pair], before)

    near = tuple(by_core(piece, "ctx", (1, 3)) for piece in (first, second))
    new_weights = last((0, 0), (first, second))
    near_first, new_weights = lax.optimization_barrier((near[0], new_weights))
    far = by_core(near_first, "ctx", (3, 1))
    cross = swapped(near[1]), swapped(near_first)
    new_weights = last((1, 3), (near_first, near[1]), new_weights)
    far, new_weights = lax.optimization_barrier((far, new_weights))
    far_too = swapped(far)
    block = jax.ShapeDtypeStruct((rank, cols), jnp.bfloat16)
    waiting = last_call(
        functools.partial(waiting_kernel, update_scale, (3, 1), (2, 2)),
        weights,
        [new_momentum, peaks, *cross, far],
        None,
        (block, block, jax.ShapeDtypeStruct((8, cols), jnp.float32)),
    )
    far_too, waiting = lax.optimization_barrier((far_too, waiting))
    closing = functools.partial(closing_kernel, update_scale, (2, 2), (3, 1))
    new_weights = last_call(closing, weights, [far, far_too, *waiting], new_weights)
    return (new_weights, new_momentum)


def solution(mesh):
    in_specs = (
        P(None, None, "fsdp"),
        P(None, None, "fsdp"),
        P(None, None, "fsdp"),
        P("dp", "ctx", None, None),
        P(),
    )
    out_specs = (P(None, None, "fsdp"), P(None, None, "fsdp"))
    return jax.shard_map(
        on_device, mesh=mesh, in_specs=in_specs, out_specs=out_specs, check_vma=False
    )
```
